32 devices in a mesh: freq: 2 (over y), dom: 16 (over z, x, core).
Axes of the slice: x: 2, y: 2, z: 4, core: 2. Of those that a mesh axis runs over, the one named last changes fastest.
Arguments:
- fwd_source: float32 [4, 4, 512, 128], P('freq', None, 'dom'), may hold values from -6 to 6
- adj_source: float32 [4, 4, 512, 128], P('freq', None, 'dom'), may hold values from -6 to 6
- curl_blocks: float32 [512, 4, 128, 128], P('dom')
- block_links: int32 [512, 4], P('dom'), may hold values from 0 to 95, as said below
- tile_lists: int32 [64, 16], P('dom'), may hold values from 0 to 31, as said below
- edge_mass: float32 [512, 128], P('dom'), may hold values from 0.5 to 1.5
- omega: float32 [4], P('freq'), may hold values from 0.1 to 1
- cell_edges: int32 [12, 16384], P(None, 'dom'), may hold values from 0 to 4095
- log_cond: float32 [16384], P('dom'), may hold values from -6 to 6
Outputs:
- fwd_field: float32 [4, 4, 512, 128], P('freq', None, 'dom')
- adj_field: float32 [4, 4, 512, 128], P('freq', None, 'dom')
- model_next: float32 [16384], P('dom')
The draws below stay inside these ranges and needn't reach their ends.
Inputs may be any that keep to these rules, and one draw needn't show every extreme that they name: `block_links`: entry 0 of each block row is the row's own local block; the others index the partition's extended field, local blocks first, then the tiles received in round 0, 1 and so on; every received tile is referenced by some row of the partition. `tile_lists`: the 16 blocks of one row are distinct local blocks.
All inputs are finite; a program needn't handle non-finite values.
Results may differ from the reference program's by a relative error of at most 0.0001.
Values sent between devices are 32-bit elements; how exact they have to be, the bound alone decides.
A program may use at most 64 MiB of HBM per device.

```python
import math
import jax
import jax.numpy as jnp
from jax import lax

EB = 128
LINKS = 4
ROUNDS = 4
ITERS = 3
NB = 32
CELLS_DEV = 1024
TILES = 16
NFREQ = 4
BLOCKS = 512
CELLS = 16384
N_DOM = 16


def draw_curl_blocks(key, part):
    noise = jax.random.normal(key, (BLOCKS, LINKS, EB, EB), jnp.float32)
    noise = noise * (0.25 / jnp.sqrt(1.0 * EB))
    eye = jnp.eye(EB, dtype=jnp.float32)
    first = (jnp.arange(LINKS) == 0).astype(jnp.float32)
    return noise + first[None, :, None, None] * eye[None, None]


def links_of_partition(key):
    slots = ROUNDS * TILES
    entries = NB * (LINKS - 1)
    fill_key, mix_key = jax.random.split(key)
    every = NB + jnp.arange(slots, dtype=jnp.int32)
    extra = jax.random.randint(fill_key, (entries - slots,), 0, NB + slots).astype(jnp.int32)
    mixed = jax.random.permutation(mix_key, jnp.concatenate([every, extra]))
    return mixed.reshape(NB, LINKS - 1)


def draw_block_links(key, part):
    keys = jax.random.split(jax.random.fold_in(key, 11), N_DOM)
    others = jax.vmap(links_of_partition)(keys).reshape(BLOCKS, LINKS - 1)
    own = (jnp.arange(BLOCKS, dtype=jnp.int32) % NB)[:, None]
    return jnp.concatenate([own, others.astype(jnp.int32)], axis=1)


def tiles_of_row(key):
    return jax.random.permutation(key, jnp.arange(NB, dtype=jnp.int32))[:TILES]


def draw_tile_lists(key, part):
    keys = jax.random.split(jax.random.fold_in(key, 23), N_DOM * ROUNDS)
    return jax.vmap(tiles_of_row)(keys).astype(jnp.int32)


def set_ends(values, own_key, least, top_value):
    index_at = [jax.random.randint(jax.random.fold_in(own_key, axis), (), 0, length) for axis, length in enumerate(values.shape)]
    main_axis = values.shape.index(max(values.shape))
    next_to = index_at[:main_axis] + [(index_at[main_axis] + 1) % values.shape[main_axis]] + index_at[main_axis + 1:]
    return values.at[tuple(index_at)].set(least).at[tuple(next_to)].set(top_value)


def levels(own_key, shape, pieces, smallest, top_value):
    loudness = 1.0
    for dim, shards_of in pieces:
        heights = jax.random.uniform(jax.random.fold_in(jax.random.fold_in(own_key, 6), dim), (shards_of,), jnp.float32, smallest / len(pieces), top_value / len(pieces))
        loudness = loudness * jnp.repeat(jnp.exp(heights), shape[dim] // shards_of).reshape((-1,) + (1,) * (len(shape) - 1 - dim))
    return loudness


def bell_draw(stream_key, shape, scale, limit, shards=(), held_as=jnp.bfloat16):
    array = jax.random.normal(stream_key, shape, jnp.float32) * scale
    if len(shards) > 0:
        array = levels(stream_key, shape, shards, -0.22, 0.18) * array
    return jnp.clip(array, min=-limit, max=limit).astype(held_as)


def setup_inputs(seed: int = 0) -> dict:
    splits = jax.random.split(jax.random.key(seed), 10)
    return {
        "fwd_source": bell_draw(splits[0], (NFREQ, 4, BLOCKS, EB), 1.0, 6.0, ((0, 2), (2, 16)), jnp.float32),
        "adj_source": bell_draw(splits[1], (NFREQ, 4, BLOCKS, EB), 1.0, 6.0, ((0, 2), (2, 16)), jnp.float32),
        "curl_blocks": draw_curl_blocks(jax.random.fold_in(splits[9], 71), 0),
        "block_links": draw_block_links(jax.random.fold_in(splits[9], 71), 0),
        "tile_lists": draw_tile_lists(jax.random.fold_in(splits[9], 71), 0),
        "edge_mass": jnp.clip(0.5 + 1.0 * jax.random.uniform(splits[5], (BLOCKS, EB), jnp.float32) ** levels(splits[5], (BLOCKS, EB), ((0, 16),), -0.2, 0.2), 0.5, 1.5),
        "omega": jnp.clip(jnp.exp(math.log(1.0) - 2.3025851 * jax.random.uniform(splits[6], (NFREQ,), jnp.float32) ** levels(splits[6], (NFREQ,), ((0, 2),), -0.2, 0.2)), 0.1, 1.0),
        "cell_edges": set_ends(jax.random.randint(splits[7], (12, CELLS), 0, NB * EB), jax.random.fold_in(splits[7], 1), 0, (NB * EB) - 1).astype(jnp.int32),
        "log_cond": bell_draw(splits[8], (CELLS,), 1.0, 6.0, ((0, 16),), jnp.float32),
    }


def apply_op(u, blocks, links, tiles, mass, omega):
    parts = [u]
    doms = jnp.arange(N_DOM, dtype=jnp.int32)
    for r in range(ROUNDS):
        partner = jnp.bitwise_xor(doms, 1 << r)
        index = tiles[partner, r]
        source = u[:, :, partner]
        got = jnp.take_along_axis(source, index[None, None, :, :, None], axis=3)
        parts.append(got)
    extended = jnp.concatenate(parts, axis=3)
    flat = links.reshape(N_DOM, NB * LINKS)
    gathered = jnp.take_along_axis(extended, flat[None, None, :, :, None], axis=3)
    gathered = gathered.reshape(u.shape[0], 4, N_DOM, NB, LINKS, EB)
    curl = jnp.einsum('dblij,fcdblj->fcdbi', blocks, gathered, precision=lax.Precision.HIGHEST)
    curl = curl.reshape(u.shape[0], 2, 2, N_DOM, NB, EB)
    split = u.reshape(u.shape[0], 2, 2, N_DOM, NB, EB)
    weight = omega[:, None, None, None, None] * mass[None, None]
    real_part = curl[:, :, 0] - weight * split[:, :, 1]
    imag_part = curl[:, :, 1] + weight * split[:, :, 0]
    return jnp.stack([real_part, imag_part], axis=2).reshape(u.shape)

def chebyshev(source, blocks, links, tiles, mass, omega):
    theta = 1.0
    delta = 0.7
    sone = theta / delta
    rho = 1.0 / sone
    solution = jnp.zeros_like(source)
    resid = source
    direction = source / theta
    for step in range(ITERS):
        solution = solution + direction
        if step + 1 < ITERS:
            resid = resid - apply_op(direction, blocks, links, tiles, mass, omega)
            rho_new = 1.0 / (2.0 * sone - rho)
            direction = rho_new * rho * direction + 2.0 * rho_new / delta * resid
            rho = rho_new
    return solution

def reference(fwd_source, adj_source, curl_blocks, block_links, tile_lists, edge_mass, omega, cell_edges, log_cond):
    blocks = curl_blocks.reshape(N_DOM, NB, LINKS, EB, EB)
    links = block_links.reshape(N_DOM, NB, LINKS)
    tiles = tile_lists.reshape(N_DOM, ROUNDS, TILES)
    mass = edge_mass.reshape(N_DOM, NB, EB)
    fwd = fwd_source.reshape(NFREQ, 4, N_DOM, NB, EB)
    adj = adj_source.reshape(NFREQ, 4, N_DOM, NB, EB)
    efield = chebyshev(fwd, blocks, links, tiles, mass, omega)
    lfield = chebyshev(adj, blocks, links, tiles, mass, omega)
    esplit = efield.reshape(NFREQ, 2, 2, N_DOM, NB * EB)
    lsplit = lfield.reshape(NFREQ, 2, 2, N_DOM, NB * EB)
    prod = esplit[:, :, 0] * lsplit[:, :, 1] + esplit[:, :, 1] * lsplit[:, :, 0]
    edge_term = lax.optimization_barrier(jnp.sum(omega[:, None, None, None] * prod, axis=(0, 1)))
    owned = cell_edges.reshape(12, N_DOM, CELLS_DEV).transpose(1, 0, 2).reshape(N_DOM, 12 * CELLS_DEV)
    picked = jnp.take_along_axis(edge_term, owned, axis=1).reshape(N_DOM, 12, CELLS_DEV)
    grad = lax.optimization_barrier(jnp.sum(picked, axis=1)).reshape(CELLS) / jnp.sqrt(24.0 * NFREQ)
    model_next = log_cond - 0.5 * grad / jnp.sqrt(grad * grad + 1.0)
    return (efield.reshape(NFREQ, 4, BLOCKS, EB), lfield.reshape(NFREQ, 4, BLOCKS, EB), model_next)
```

```python
import functools

import jax
import jax.numpy as jnp
from jax import lax
from jax.experimental import pallas as pl
from jax.experimental.pallas import tpu as pltpu
from jax.sharding import PartitionSpec as P

THETA = 1.0
DELTA = 0.7
MESH = pl.DeviceIdType.MESH
CHUNK = 4
UNROLL = 4


def chebyshev_factors():
    sone = THETA / DELTA
    rho = 1.0 / sone
    factors = []
    for _ in range(2):
        rho_new = 1.0 / (2.0 * sone - rho)
        factors.append((rho_new * rho, 2.0 * rho_new / DELTA))
        rho = rho_new
    return factors


def split(value):
    high = value.astype(jnp.bfloat16)
    low = (value - high.astype(jnp.float32)).astype(jnp.bfloat16)
    return high, low


def row_of(count, system, f, c):
    return (c % 2) * 4 * count + system * 2 * count + f * 2 + c // 2


def kernel(
    peers,
    links_ref,
    tiles_ref,
    omega_ref,
    fwd_ref,
    adj_ref,
    curl_ref,
    mass_ref,
    total,
    edge_out,
    raw,
    parts,
    first,
    second,
    resid,
    ext_one,
    ext_two,
    send_one,
    send_two,
    terms,
    raw_sem,
    send_sem,
    recv_sem,
    term_send_sem,
    term_recv_sem,
):
    blocks = mass_ref.shape[0]
    count = fwd_ref.shape[0]
    width = 8 * count
    half = width // 2
    rounds, tiles = tiles_ref.shape
    links = links_ref.shape[1]
    size = mass_ref.shape[1]
    freq = lax.axis_index("freq")
    dom = lax.axis_index("dom")

    def raw_copy(chunk):
        rows = pl.ds(chunk * CHUNK, CHUNK)
        return pltpu.make_async_copy(curl_ref.at[rows], raw.at[rows], raw_sem.at[chunk])

    for chunk in range(blocks // CHUNK):
        raw_copy(chunk).start()

    partners = []
    for bit in range(rounds):
        mask = 2**bit
        partners.append((freq, dom + mask * (1 - 2 * ((dom // mask) % 2))))
    others = [(lax.rem(freq + step, peers), dom) for step in range(1, peers)]

    barrier = pltpu.get_barrier_semaphore()
    for device in partners + others:
        pl.semaphore_signal(barrier, inc=1, device_id=device, device_id_type=MESH)

    for system, ref in enumerate((fwd_ref, adj_ref)):
        for f in range(count):
            for c in range(4):
                first[:, row_of(count, system, f, c), :] = ref[f, c]

    def exchange(field, send, ext, phase):
        copies = []
        for bit in reversed(range(rounds)):
            for tile in range(tiles):
                send[bit * tiles + tile] = field[tiles_ref[bit, tile]]
            if phase == 0 and bit == rounds - 1:
                pl.semaphore_wait(barrier, len(partners) + len(others))
            copy = pltpu.make_async_remote_copy(
                src_ref=send.at[pl.ds(bit * tiles, tiles)],
                dst_ref=ext.at[pl.ds(blocks + bit * tiles, tiles)],
                send_sem=send_sem.at[phase, bit],
                recv_sem=recv_sem.at[phase, bit],
                device_id=partners[bit],
                device_id_type=MESH,
            )
            copy.start()
            copies.append(copy)
        return copies

    copies = exchange(first, send_one, ext_one, 0)
    ext_one[pl.ds(0, blocks)] = first[...]

    for chunk in range(blocks // CHUNK):
        raw_copy(chunk).wait()

        def cut(step, carry):
            row = chunk * CHUNK + step
            for link in range(links):
                high, low = split(raw[row, link])
                columns = pl.ds(link * size, size)
                parts[row, pl.ds(0, size), columns] = high
                parts[row, pl.ds(size, size), columns] = low
            return carry

        lax.fori_loop(0, CHUNK, cut, 0)

    place = lax.broadcasted_iota(jnp.int32, (half, size), 0)
    place = lax.rem(place // 2, count)
    omega = jnp.zeros((half, size), jnp.float32)
    for f in range(count):
        omega = jnp.where(place == f, omega_ref[f], omega)

    def operate(row, field, ext):
        gathered = [ext[links_ref[row, link]] for link in range(links)]
        high, low = split(jnp.concatenate(gathered, axis=1))
        both = jnp.concatenate([high, low], axis=0)
        product = lax.dot_general(
            both, parts[row], (((1,), (1,)), ((), ())), preferred_element_type=jnp.float32
        )
        product = product[:width] + product[width:]
        curl = product[:, :size] + product[:, size:]
        weight = omega * mass_ref[pl.ds(row, 1), :]
        real = field[row, pl.ds(0, half)]
        imag = field[row, pl.ds(half, half)]
        return real, imag, curl[:half] - weight * imag, curl[half:] + weight * real

    factors = chebyshev_factors()

    for copy in copies:
        copy.wait()

    def one(step, carry):
        keep, gain = factors[0]
        for inner in range(UNROLL):
            row = step * UNROLL + inner
            real, imag, image_real, image_imag = operate(row, first, ext_one)
            for value, image, start in ((real, image_real, 0), (imag, image_imag, half)):
                left = value - image
                resid[row, pl.ds(start, half)] = left
                second[row, pl.ds(start, half)] = keep * value + gain * left
        return carry

    lax.fori_loop(0, blocks // UNROLL, one, 0)

    copies = exchange(second, send_two, ext_two, 1)
    ext_two[pl.ds(0, blocks)] = second[...]
    for copy in copies:
        copy.wait()

    def two(step, carry):
        keep, gain = factors[1]
        for inner in range(UNROLL):
            row = step * UNROLL + inner
            real, imag, image_real, image_imag = operate(row, second, ext_two)
            done = []
            for value, image, start in ((real, image_real, 0), (imag, image_imag, half)):
                left = resid[row, pl.ds(start, half)] - image
                step_three = keep * value + gain * left
                done.append((first[row, pl.ds(start, half)] + value) + step_three)
                total[row, pl.ds(start, half)] = done[-1]
            crossed = jnp.concatenate([done[1][half // 2 :], done[1][: half // 2]], axis=0)
            term = omega * done[0] * crossed
            terms[freq, pl.ds(row, 1), :] = jnp.sum(term, axis=0, keepdims=True)
        return carry

    lax.fori_loop(0, blocks // UNROLL, two, 0)

    copies = []
    for step in range(1, peers):
        copy = pltpu.make_async_remote_copy(
            src_ref=terms.at[freq],
            dst_ref=terms.at[freq],
            send_sem=term_send_sem.at[step],
            recv_sem=term_recv_sem.at[step],
            device_id=others[step - 1],
            device_id_type=MESH,
        )
        copy.start()
        copies.append(copy)
    for copy in copies:
        copy.wait()
    whole = terms[0]
    for peer in range(1, peers):
        whole = whole + terms[peer]
    edge_out[...] = whole


def finish(scale, total_ref, edge_ref, cells_ref, cond_ref, fwd_out, adj_out, model_out):
    blocks, size = edge_ref.shape
    count = fwd_out.shape[0]
    width = 8 * count
    for system, ref in enumerate((fwd_out, adj_out)):
        for f in range(count):
            for c in range(4):
                row = row_of(count, system, f, c)
                ref[f, c] = total_ref[:, row, :]

    corners, cells = cells_ref.shape
    shift = size.bit_length() - 1
    sums = []
    for column in range(cells // size):
        acc = jnp.zeros((1, size), jnp.float32)
        for start in range(0, corners, 8):
            rows = min(8, corners - start)
            ids = cells_ref[pl.ds(start, rows), pl.ds(column * size, size)]
            if rows < 8:
                ids = jnp.concatenate([ids, jnp.full((8 - rows, size), -1, jnp.int32)], axis=0)
            block = ids >> shift
            lane = ids & (size - 1)
            found = jnp.zeros((8, size), jnp.float32)
            for row in range(blocks):
                values = jnp.broadcast_to(edge_ref[pl.ds(row, 1), :], (8, size))
                got = jnp.take_along_axis(values, lane, axis=1, mode="promise_in_bounds")
                found = jnp.where(block == row, got, found)
            acc = acc + jnp.sum(found, axis=0, keepdims=True)
        sums.append(acc)
    grad = jnp.concatenate(sums, axis=0) * scale
    model_out[...] = cond_ref[...] - 0.5 * grad / jnp.sqrt(grad * grad + 1.0)


def local(
    fwd_source,
    adj_source,
    curl_blocks,
    block_links,
    tile_lists,
    edge_mass,
    omega,
    cell_edges,
    log_cond,
):
    count, _, blocks, size = fwd_source.shape
    peers = lax.axis_size("freq")
    width = 8 * count
    rounds, tiles = tile_lists.shape
    sent = rounds * tiles
    links = block_links.shape[1]
    cells = log_cond.shape[0]
    cond = log_cond.reshape(cells // size, size)
    f32, bf16 = jnp.float32, jnp.bfloat16
    vmem = pl.BlockSpec(memory_space=pltpu.VMEM)
    smem = pl.BlockSpec(memory_space=pltpu.SMEM)
    total, edge = pl.pallas_call(
        functools.partial(kernel, peers),
        out_shape=(
            jax.ShapeDtypeStruct((blocks, width, size), f32),
            jax.ShapeDtypeStruct((blocks, size), f32),
        ),
        in_specs=[smem, smem, smem, vmem, vmem, pl.BlockSpec(memory_space=pl.ANY), vmem],
        out_specs=(vmem, vmem),
        scratch_shapes=[
            pltpu.VMEM(curl_blocks.shape, f32),
            pltpu.VMEM((blocks, 2 * size, links * size), bf16),
            pltpu.VMEM((blocks, width, size), f32),
            pltpu.VMEM((blocks, width, size), f32),
            pltpu.VMEM((blocks, width, size), f32),
            pltpu.VMEM((blocks + sent, width, size), f32),
            pltpu.VMEM((blocks + sent, width, size), f32),
            pltpu.VMEM((sent, width, size), f32),
            pltpu.VMEM((sent, width, size), f32),
            pltpu.VMEM((peers, blocks, size), f32),
            pltpu.SemaphoreType.DMA((blocks // CHUNK,)),
            pltpu.SemaphoreType.DMA((2, rounds)),
            pltpu.SemaphoreType.DMA((2, rounds)),
            pltpu.SemaphoreType.DMA((peers,)),
            pltpu.SemaphoreType.DMA((peers,)),
        ],
        compiler_params=pltpu.CompilerParams(
            collective_id=0, has_side_effects=True, vmem_limit_bytes=48 * 1024 * 1024
        ),
    )(block_links, tile_lists, omega, fwd_source, adj_source, curl_blocks, edge_mass)
    scale = 1.0 / (24.0 * count * peers) ** 0.5
    fwd_field, adj_field, model = pl.pallas_call(
        functools.partial(finish, scale),
        out_shape=(
            jax.ShapeDtypeStruct(fwd_source.shape, f32),
            jax.ShapeDtypeStruct(adj_source.shape, f32),
            jax.ShapeDtypeStruct(cond.shape, f32),
        ),
        in_specs=[vmem] * 4,
        out_specs=(vmem,) * 3,
    )(total, edge, cell_edges, cond)
    return fwd_field, adj_field, model.reshape(cells)


def solution(mesh):
    in_specs = (
        P("freq", None, "dom", None),
        P("freq", None, "dom", None),
        P("dom", None, None, None),
        P("dom", None),
        P("dom", None),
        P("dom", None),
        P("freq"),
        P(None, "dom"),
        P("dom"),
    )
    out_specs = (P("freq", None, "dom", None), P("freq", None, "dom", None), P("dom"))
    return jax.shard_map(local, mesh=mesh, in_specs=in_specs, out_specs=out_specs, check_vma=False)
```

```python
import functools

import jax
import jax.numpy as jnp
from jax import lax
from jax.experimental import pallas as pl
from jax.experimental.pallas import tpu as pltpu
from jax.sharding import PartitionSpec as P

THETA = 1.0
DELTA = 0.7
MESH = pl.DeviceIdType.MESH
VMEM = 63 * 1024 * 1024
CHUNK = 4
UNROLL = 4


def chebyshev_factors():
    sone = THETA / DELTA
    rho = 1.0 / sone
    factors = []
    for _ in range(2):
        rho_new = 1.0 / (2.0 * sone - rho)
        factors.append((rho_new * rho, 2.0 * rho_new / DELTA))
        rho = rho_new
    return factors


def split(value):
    high = value.astype(jnp.bfloat16)
    low = (value - high.astype(jnp.float32)).astype(jnp.bfloat16)
    return high, low


def row_of(count, system, f, c):
    return (c % 2) * 4 * count + system * 2 * count + f * 2 + c // 2


def kernel(
    peers,
    links_hbm,
    tiles_hbm,
    omega_hbm,
    fwd_hbm,
    adj_hbm,
    curl_hbm,
    mass_hbm,
    fwd_out,
    adj_out,
    edge_out,
    links_ref,
    tiles_ref,
    omega_ref,
    fwd_ref,
    adj_ref,
    mass_ref,
    raw,
    parts,
    weight,
    first,
    second,
    resid,
    total,
    ext_one,
    ext_two,
    send_one,
    send_two,
    terms,
    load_sem,
    raw_sem,
    send_sem,
    recv_sem,
    term_send_sem,
    term_recv_sem,
):
    blocks, size = mass_ref.shape
    count = fwd_ref.shape[0]
    width = 8 * count
    half = width // 2
    rounds, tiles = tiles_ref.shape
    links = links_ref.shape[0]
    freq = lax.axis_index("freq")
    dom = lax.axis_index("dom")

    loads = {}
    for at, (name, source, target) in enumerate(
        (
            ("fwd", fwd_hbm, fwd_ref),
            ("adj", adj_hbm, adj_ref),
            ("tiles", tiles_hbm, tiles_ref),
            ("links", links_hbm, links_ref),
            ("omega", omega_hbm, omega_ref),
            ("mass", mass_hbm, mass_ref),
        )
    ):
        loads[name] = pltpu.make_async_copy(source, target, load_sem.at[at])
        loads[name].start()

    def raw_copy(chunk):
        rows = pl.ds(chunk * CHUNK, CHUNK)
        return pltpu.make_async_copy(curl_hbm.at[rows], raw.at[rows], raw_sem.at[chunk])

    for chunk in range(blocks // CHUNK):
        raw_copy(chunk).start()

    partners = []
    for bit in range(rounds):
        mask = 2**bit
        partners.append((freq, dom + mask * (1 - 2 * ((dom // mask) % 2))))
    others = [(lax.rem(freq + step, peers), dom) for step in range(1, peers)]

    barrier = pltpu.get_barrier_semaphore()
    for device in partners + others:
        pl.semaphore_signal(barrier, inc=1, device_id=device, device_id_type=MESH)

    for system, (name, ref) in enumerate((("fwd", fwd_ref), ("adj", adj_ref))):
        loads[name].wait()
        for f in range(count):
            for c in range(4):
                first[:, row_of(count, system, f, c), :] = ref[f, c]

    pieces = 2
    span = tiles // pieces

    def push(send, ext, phase, bit, piece):
        rows = bit * tiles + piece * span
        copy = pltpu.make_async_remote_copy(
            src_ref=send.at[pl.ds(rows, span)],
            dst_ref=ext.at[pl.ds(blocks + rows, span)],
            send_sem=send_sem.at[phase, bit, piece],
            recv_sem=recv_sem.at[phase, bit, piece],
            device_id=partners[bit],
            device_id_type=MESH,
        )
        copy.start()
        return copy

    loads["tiles"].wait()
    copies = []
    for bit in reversed(range(rounds)):
        for piece in range(pieces):
            for tile in range(piece * span, (piece + 1) * span):
                send_one[bit * tiles + tile] = first[tiles_ref[bit, tile]]
            if len(copies) == 0:
                pl.semaphore_wait(barrier, len(partners) + len(others))
            copies.append(push(send_one, ext_one, 0, bit, piece))
    ext_one[pl.ds(0, blocks)] = first[...]

    for name in ("links", "omega", "mass"):
        loads[name].wait()
    place = lax.broadcasted_iota(jnp.int32, (half, size), 0)
    place = lax.rem(place // 2, count)
    omega = jnp.zeros((half, size), jnp.float32)
    for f in range(count):
        omega = jnp.where(place == f, omega_ref[f], omega)
    for row in range(blocks):
        weight[row] = omega * mass_ref[pl.ds(row, 1), :]

    for chunk in range(blocks // CHUNK):
        raw_copy(chunk).wait()

        def cut(step, carry):
            row = chunk * CHUNK + step
            for link in range(links):
                high, low = split(raw[row, link])
                columns = pl.ds(link * size, size)
                parts[row, pl.ds(0, size), columns] = high
                parts[row, pl.ds(size, size), columns] = low
            return carry

        lax.fori_loop(0, CHUNK, cut, 0)

    def operate(row, field, ext):
        gathered = [ext[links_ref[link, row]] for link in range(links)]
        high, low = split(jnp.concatenate(gathered, axis=1))
        both = jnp.concatenate([high, low], axis=0)
        product = lax.dot_general(
            both, parts[row], (((1,), (1,)), ((), ())), preferred_element_type=jnp.float32
        )
        product = product[:width] + product[width:]
        curl = product[:, :size] + product[:, size:]
        value = field[row]
        turned = jnp.concatenate([-value[half:], value[:half]], axis=0)
        scale = weight[row]
        return value, curl + jnp.concatenate([scale, scale], axis=0) * turned

    factors = chebyshev_factors()

    def advance(row):
        keep, gain = factors[0]
        value, image = operate(row, first, ext_one)
        left = value - image
        return left, keep * value + gain * left

    for copy in copies:
        copy.wait()

    copies = []
    for bit in reversed(range(rounds)[-2:]):
        for piece in range(pieces):

            def ahead(step, carry):
                for inner in range(UNROLL):
                    tile = piece * span + step * UNROLL + inner
                    send_two[bit * tiles + tile] = advance(tiles_ref[bit, tile])[1]
                return carry

            lax.fori_loop(0, span // UNROLL, ahead, 0)
            copies.append(push(send_two, ext_two, 1, bit, piece))

    def one(step, carry):
        for inner in range(UNROLL):
            row = step * UNROLL + inner
            left, value = advance(row)
            resid[row] = left
            second[row] = value
        return carry

    lax.fori_loop(0, blocks // UNROLL, one, 0)
    for bit in reversed(range(rounds)[:-2]):
        for piece in range(pieces):
            for tile in range(piece * span, (piece + 1) * span):
                send_two[bit * tiles + tile] = second[tiles_ref[bit, tile]]
            copies.append(push(send_two, ext_two, 1, bit, piece))
    ext_two[pl.ds(0, blocks)] = second[...]
    for copy in copies:
        copy.wait()

    def two(step, carry):
        keep, gain = factors[1]
        for inner in range(UNROLL):
            row = step * UNROLL + inner
            value, image = operate(row, second, ext_two)
            left = resid[row] - image
            done = (first[row] + value) + (keep * value + gain * left)
            total[row] = done
            crossed = jnp.concatenate([done[half + half // 2 :], done[half : half + half // 2]], axis=0)
            term = omega * done[:half] * crossed
            terms[freq, pl.ds(row, 1), :] = jnp.sum(term, axis=0, keepdims=True)
        return carry

    lax.fori_loop(0, blocks // UNROLL, two, 0)

    copies = []
    for step in range(1, peers):
        copy = pltpu.make_async_remote_copy(
            src_ref=terms.at[freq],
            dst_ref=terms.at[freq],
            send_sem=term_send_sem.at[step],
            recv_sem=term_recv_sem.at[step],
            device_id=others[step - 1],
            device_id_type=MESH,
        )
        copy.start()
        copies.append(copy)
    for system, ref in enumerate((fwd_ref, adj_ref)):
        for f in range(count):
            for c in range(4):
                ref[f, c] = total[:, row_of(count, system, f, c), :]
    stores = []
    for at, (source, target) in enumerate(((fwd_ref, fwd_out), (adj_ref, adj_out))):
        stores.append(pltpu.make_async_copy(source, target, load_sem.at[6 + at]))
        stores[-1].start()
    for copy in copies:
        copy.wait()
    whole = terms[0]
    for peer in range(1, peers):
        whole = whole + terms[peer]
    mass_ref[...] = whole
    stores.append(pltpu.make_async_copy(mass_ref, edge_out, load_sem.at[8]))
    stores[-1].start()
    for copy in stores:
        copy.wait()


def finish(
    scale,
    fwd_hbm,
    adj_hbm,
    edge_hbm,
    cells_hbm,
    cond_hbm,
    fwd_out,
    adj_out,
    model_out,
    edge_ref,
    cells_ref,
    cond_ref,
    copy_sem,
):
    pairs = (
        (edge_hbm, edge_ref),
        (cells_hbm, cells_ref),
        (cond_hbm, cond_ref),
        (fwd_hbm, fwd_out),
        (adj_hbm, adj_out),
    )
    copies = []
    for at, (source, target) in enumerate(pairs):
        copies.append(pltpu.make_async_copy(source, target, copy_sem.at[at]))
        copies[-1].start()
    for copy in copies[:3]:
        copy.wait()

    blocks, size = edge_ref.shape
    corners, cells = cells_ref.shape
    shift = size.bit_length() - 1
    sums = []
    for column in range(cells // size):
        acc = jnp.zeros((1, size), jnp.float32)
        for start in range(0, corners, 8):
            rows = min(8, corners - start)
            ids = cells_ref[pl.ds(start, rows), pl.ds(column * size, size)]
            if rows < 8:
                ids = jnp.concatenate([ids, jnp.full((8 - rows, size), -1, jnp.int32)], axis=0)
            block = ids >> shift
            lane = ids & (size - 1)
            found = jnp.zeros((8, size), jnp.float32)
            for row in range(blocks):
                values = jnp.broadcast_to(edge_ref[pl.ds(row, 1), :], (8, size))
                got = jnp.take_along_axis(values, lane, axis=1, mode="promise_in_bounds")
                found = jnp.where(block == row, got, found)
            acc = acc + jnp.sum(found, axis=0, keepdims=True)
        sums.append(acc)
    grad = jnp.concatenate(sums, axis=0) * scale
    model_out[...] = cond_ref[...] - 0.5 * grad / jnp.sqrt(grad * grad + 1.0)
    for copy in copies[3:]:
        copy.wait()


def local(
    fwd_source,
    adj_source,
    curl_blocks,
    block_links,
    tile_lists,
    edge_mass,
    omega,
    cell_edges,
    log_cond,
):
    count, _, blocks, size = fwd_source.shape
    peers = lax.axis_size("freq")
    width = 8 * count
    rounds, tiles = tile_lists.shape
    sent = rounds * tiles
    links = block_links.shape[1]
    cells = log_cond.shape[0]
    cond = log_cond.reshape(cells // size, size)
    f32, bf16 = jnp.float32, jnp.bfloat16
    vmem = pl.BlockSpec(memory_space=pltpu.VMEM)
    hbm = pl.BlockSpec(memory_space=pltpu.HBM)
    fields, adjoint, edge = pl.pallas_call(
        functools.partial(kernel, peers),
        out_shape=(
            jax.ShapeDtypeStruct(fwd_source.shape, f32),
            jax.ShapeDtypeStruct(adj_source.shape, f32),
            jax.ShapeDtypeStruct((blocks, size), f32),
        ),
        in_specs=[hbm] * 7,
        out_specs=(hbm,) * 3,
        scratch_shapes=[
            pltpu.SMEM((links, blocks), jnp.int32),
            pltpu.SMEM((rounds, tiles), jnp.int32),
            pltpu.SMEM((count,), f32),
            pltpu.VMEM(fwd_source.shape, f32),
            pltpu.VMEM(adj_source.shape, f32),
            pltpu.VMEM((blocks, size), f32),
            pltpu.VMEM(curl_blocks.shape, f32),
            pltpu.VMEM((blocks, 2 * size, links * size), bf16),
            pltpu.VMEM((blocks, width // 2, size), f32),
            pltpu.VMEM((blocks, width, size), f32),
            pltpu.VMEM((blocks, width, size), f32),
            pltpu.VMEM((blocks, width, size), f32),
            pltpu.VMEM((blocks, width, size), f32),
            pltpu.VMEM((blocks + sent, width, size), f32),
            pltpu.VMEM((blocks + sent, width, size), f32),
            pltpu.VMEM((sent, width, size), f32),
            pltpu.VMEM((sent, width, size), f32),
            pltpu.VMEM((peers, blocks, size), f32),
            pltpu.SemaphoreType.DMA((9,)),
            pltpu.SemaphoreType.DMA((blocks // CHUNK,)),
            pltpu.SemaphoreType.DMA((2, rounds, 2)),
            pltpu.SemaphoreType.DMA((2, rounds, 2)),
            pltpu.SemaphoreType.DMA((peers,)),
            pltpu.SemaphoreType.DMA((peers,)),
        ],
        compiler_params=pltpu.CompilerParams(
            collective_id=0, has_side_effects=True, vmem_limit_bytes=VMEM
        ),
    )(
        block_links.T,
        tile_lists,
        omega,
        fwd_source,
        adj_source,
        curl_blocks,
        edge_mass,
    )
    scale = 1.0 / (24.0 * count * peers) ** 0.5
    fwd_field, adj_field, model = pl.pallas_call(
        functools.partial(finish, scale),
        out_shape=(
            jax.ShapeDtypeStruct(fwd_source.shape, f32),
            jax.ShapeDtypeStruct(adj_source.shape, f32),
            jax.ShapeDtypeStruct(cond.shape, f32),
        ),
        in_specs=[hbm] * 5,
        out_specs=(hbm, hbm, vmem),
        scratch_shapes=[
            pltpu.VMEM((blocks, size), f32),
            pltpu.VMEM(cell_edges.shape, jnp.int32),
            pltpu.VMEM(cond.shape, f32),
            pltpu.SemaphoreType.DMA((5,)),
        ],
        compiler_params=pltpu.CompilerParams(vmem_limit_bytes=VMEM),
    )(fields, adjoint, edge, cell_edges, cond)
    return fwd_field, adj_field, model.reshape(cells)


def solution(mesh):
    in_specs = (
        P("freq", None, "dom", None),
        P("freq", None, "dom", None),
        P("dom", None, None, None),
        P("dom", None),
        P("dom", None),
        P("dom", None),
        P("freq"),
        P(None, "dom"),
        P("dom"),
    )
    out_specs = (P("freq", None, "dom", None), P("freq", None, "dom", None), P("dom"))
    return jax.shard_map(local, mesh=mesh, in_specs=in_specs, out_specs=out_specs, check_vma=False)
```

```python
import functools

import jax
import jax.numpy as jnp
from jax import lax
from jax.experimental import pallas as pl
from jax.experimental.pallas import tpu as pltpu
from jax.sharding import PartitionSpec as P

THETA = 1.0
DELTA = 0.7
MESH = pl.DeviceIdType.MESH
VMEM = 63 * 1024 * 1024
CHUNK = 4
UNROLL = 4


def chebyshev_factors():
    sone = THETA / DELTA
    rho = 1.0 / sone
    factors = []
    for _ in range(2):
        rho_new = 1.0 / (2.0 * sone - rho)
        factors.append((rho_new * rho, 2.0 * rho_new / DELTA))
        rho = rho_new
    return factors


def split(value):
    high = value.astype(jnp.bfloat16)
    low = (value - high.astype(jnp.float32)).astype(jnp.bfloat16)
    return high, low


def row_of(count, system, f, c):
    return (c % 2) * 4 * count + system * 2 * count + f * 2 + c // 2


def kernel(
    peers,
    links_hbm,
    tiles_hbm,
    omega_hbm,
    fwd_hbm,
    adj_hbm,
    curl_hbm,
    mass_hbm,
    fwd_out,
    adj_out,
    edge_out,
    links_ref,
    tiles_ref,
    omega_ref,
    fwd_ref,
    adj_ref,
    mass_ref,
    raw,
    parts,
    weight,
    first,
    second,
    resid,
    total,
    ext_one,
    ext_two,
    send_one,
    send_two,
    terms,
    load_sem,
    raw_sem,
    send_sem,
    recv_sem,
    term_send_sem,
    term_recv_sem,
):
    blocks, size = mass_ref.shape
    count = fwd_ref.shape[0]
    width = 8 * count
    half = width // 2
    rounds, tiles = tiles_ref.shape
    links = links_ref.shape[0]
    freq = lax.axis_index("freq")
    dom = lax.axis_index("dom")

    loads = {}
    for at, (name, source, target) in enumerate(
        (
            ("fwd", fwd_hbm, fwd_ref),
            ("adj", adj_hbm, adj_ref),
            ("tiles", tiles_hbm, tiles_ref),
            ("links", links_hbm, links_ref),
            ("omega", omega_hbm, omega_ref),
            ("mass", mass_hbm, mass_ref),
        )
    ):
        loads[name] = pltpu.make_async_copy(source, target, load_sem.at[at])
        loads[name].start()

    def raw_copy(chunk):
        rows = pl.ds(chunk * CHUNK, CHUNK)
        return pltpu.make_async_copy(curl_hbm.at[rows], raw.at[rows], raw_sem.at[chunk])

    for chunk in range(blocks // CHUNK):
        raw_copy(chunk).start()

    partners = []
    for bit in range(rounds):
        mask = 2**bit
        partners.append((freq, dom + mask * (1 - 2 * ((dom // mask) % 2))))
    others = [(lax.rem(freq + step, peers), dom) for step in range(1, peers)]

    barrier = pltpu.get_barrier_semaphore()
    for device in partners + others:
        pl.semaphore_signal(barrier, inc=1, device_id=device, device_id_type=MESH)

    for system, (name, ref) in enumerate((("fwd", fwd_ref), ("adj", adj_ref))):
        loads[name].wait()
        for f in range(count):
            for c in range(4):
                first[:, row_of(count, system, f, c), :] = ref[f, c]

    pieces = 2
    span = tiles // pieces

    def push(send, ext, phase, bit, piece):
        rows = bit * tiles + piece * span
        copy = pltpu.make_async_remote_copy(
            src_ref=send.at[pl.ds(rows, span)],
            dst_ref=ext.at[pl.ds(blocks + rows, span)],
            send_sem=send_sem.at[phase, bit, piece],
            recv_sem=recv_sem.at[phase, bit, piece],
            device_id=partners[bit],
            device_id_type=MESH,
        )
        copy.start()
        return copy

    loads["tiles"].wait()
    copies = []
    for bit in reversed(range(rounds)):
        for piece in range(pieces):
            for tile in range(piece * span, (piece + 1) * span):
                send_one[bit * tiles + tile] = first[tiles_ref[bit, tile]]
            if len(copies) == 0:
                pl.semaphore_wait(barrier, len(partners) + len(others))
            copies.append(push(send_one, ext_one, 0, bit, piece))
    ext_one[pl.ds(0, blocks)] = first[...]

    for name in ("links", "omega", "mass"):
        loads[name].wait()
    place = lax.broadcasted_iota(jnp.int32, (half, size), 0)
    place = lax.rem(place // 2, count)
    omega = jnp.zeros((half, size), jnp.float32)
    for f in range(count):
        omega = jnp.where(place == f, omega_ref[f], omega)
    for row in range(blocks):
        weight[row] = omega * mass_ref[pl.ds(row, 1), :]

    for chunk in range(blocks // CHUNK):
        raw_copy(chunk).wait()

        def cut(step, carry):
            row = chunk * CHUNK + step
            for link in range(links):
                high, low = split(raw[row, link].T)
                rows = pl.ds(link * size, size)
                parts[row, rows, pl.ds(0, size)] = high
                parts[row, rows, pl.ds(size, size)] = low
            return carry

        lax.fori_loop(0, CHUNK, cut, 0)

    def operate(row, field, ext):
        gathered = [ext[links_ref[link, row]] for link in range(links)]
        high, low = split(jnp.concatenate(gathered, axis=1))
        both = jnp.concatenate([high, low], axis=0)
        product = jnp.dot(both, parts[row], preferred_element_type=jnp.float32)
        product = product[:width] + product[width:]
        curl = product[:, :size] + product[:, size:]
        value = field[row]
        turned = jnp.concatenate([-value[half:], value[:half]], axis=0)
        scale = weight[row]
        return value, curl + jnp.concatenate([scale, scale], axis=0) * turned

    factors = chebyshev_factors()

    def advance(row):
        keep, gain = factors[0]
        value, image = operate(row, first, ext_one)
        left = value - image
        return left, keep * value + gain * left

    for copy in copies:
        copy.wait()

    copies = []
    for bit in reversed(range(rounds)[-2:]):
        for piece in range(pieces):

            def ahead(step, carry):
                for inner in range(UNROLL):
                    tile = piece * span + step * UNROLL + inner
                    send_two[bit * tiles + tile] = advance(tiles_ref[bit, tile])[1]
                return carry

            lax.fori_loop(0, span // UNROLL, ahead, 0)
            copies.append(push(send_two, ext_two, 1, bit, piece))

    def one(step, carry):
        for inner in range(UNROLL):
            row = step * UNROLL + inner
            left, value = advance(row)
            resid[row] = left
            second[row] = value
        return carry

    lax.fori_loop(0, blocks // UNROLL, one, 0)
    for bit in reversed(range(rounds)[:-2]):
        for piece in range(pieces):
            for tile in range(piece * span, (piece + 1) * span):
                send_two[bit * tiles + tile] = second[tiles_ref[bit, tile]]
            copies.append(push(send_two, ext_two, 1, bit, piece))
    ext_two[pl.ds(0, blocks)] = second[...]
    for copy in copies:
        copy.wait()

    def two(step, carry):
        keep, gain = factors[1]
        for inner in range(UNROLL):
            row = step * UNROLL + inner
            value, image = operate(row, second, ext_two)
            left = resid[row] - image
            done = (first[row] + value) + (keep * value + gain * left)
            total[row] = done
            crossed = jnp.concatenate([done[half + half // 2 :], done[half : half + half // 2]], axis=0)
            term = omega * done[:half] * crossed
            terms[freq, pl.ds(row, 1), :] = jnp.sum(term, axis=0, keepdims=True)
        return carry

    lax.fori_loop(0, blocks // UNROLL, two, 0)

    copies = []
    for step in range(1, peers):
        copy = pltpu.make_async_remote_copy(
            src_ref=terms.at[freq],
            dst_ref=terms.at[freq],
            send_sem=term_send_sem.at[step],
            recv_sem=term_recv_sem.at[step],
            device_id=others[step - 1],
            device_id_type=MESH,
        )
        copy.start()
        copies.append(copy)
    for system, ref in enumerate((fwd_ref, adj_ref)):
        for f in range(count):
            for c in range(4):
                ref[f, c] = total[:, row_of(count, system, f, c), :]
    stores = []
    for at, (source, target) in enumerate(((fwd_ref, fwd_out), (adj_ref, adj_out))):
        stores.append(pltpu.make_async_copy(source, target, load_sem.at[6 + at]))
        stores[-1].start()
    for copy in copies:
        copy.wait()
    whole = terms[0]
    for peer in range(1, peers):
        whole = whole + terms[peer]
    mass_ref[...] = whole
    stores.append(pltpu.make_async_copy(mass_ref, edge_out, load_sem.at[8]))
    stores[-1].start()
    for copy in stores:
        copy.wait()


def finish(
    scale,
    fwd_hbm,
    adj_hbm,
    edge_hbm,
    cells_hbm,
    cond_hbm,
    fwd_out,
    adj_out,
    model_out,
    edge_ref,
    cells_ref,
    cond_ref,
    fwd_ref,
    adj_ref,
    copy_sem,
):
    pairs = (
        (edge_hbm, edge_ref),
        (cells_hbm, cells_ref),
        (cond_hbm, cond_ref),
        (fwd_hbm, fwd_ref),
        (adj_hbm, adj_ref),
        (fwd_ref, fwd_out),
        (adj_ref, adj_out),
    )
    copies = [pltpu.make_async_copy(*pair, copy_sem.at[at]) for at, pair in enumerate(pairs)]
    for copy in copies[:5]:
        copy.start()
    for copy in copies[:5]:
        copy.wait()
    for copy in copies[5:]:
        copy.start()

    blocks, size = edge_ref.shape
    corners, cells = cells_ref.shape
    shift = size.bit_length() - 1
    sums = []
    for column in range(cells // size):
        acc = jnp.zeros((1, size), jnp.float32)
        for start in range(0, corners, 8):
            rows = min(8, corners - start)
            ids = cells_ref[pl.ds(start, rows), pl.ds(column * size, size)]
            if rows < 8:
                ids = jnp.concatenate([ids, jnp.full((8 - rows, size), -1, jnp.int32)], axis=0)
            block = ids >> shift
            lane = ids & (size - 1)
            found = jnp.zeros((8, size), jnp.float32)
            for row in range(blocks):
                values = jnp.broadcast_to(edge_ref[pl.ds(row, 1), :], (8, size))
                got = jnp.take_along_axis(values, lane, axis=1, mode="promise_in_bounds")
                found = jnp.where(block == row, got, found)
            acc = acc + jnp.sum(found, axis=0, keepdims=True)
        sums.append(acc)
    grad = jnp.concatenate(sums, axis=0) * scale
    model_out[...] = cond_ref[...] - 0.5 * grad / jnp.sqrt(grad * grad + 1.0)
    for copy in copies[5:]:
        copy.wait()


def local(
    fwd_source,
    adj_source,
    curl_blocks,
    block_links,
    tile_lists,
    edge_mass,
    omega,
    cell_edges,
    log_cond,
):
    count, _, blocks, size = fwd_source.shape
    peers = lax.axis_size("freq")
    width = 8 * count
    rounds, tiles = tile_lists.shape
    sent = rounds * tiles
    links = block_links.shape[1]
    cells = log_cond.shape[0]
    cond = log_cond.reshape(cells // size, size)
    f32, bf16 = jnp.float32, jnp.bfloat16
    vmem = pl.BlockSpec(memory_space=pltpu.VMEM)
    hbm = pl.BlockSpec(memory_space=pltpu.HBM)
    fields, adjoint, edge = pl.pallas_call(
        functools.partial(kernel, peers),
        out_shape=(
            jax.ShapeDtypeStruct(fwd_source.shape, f32),
            jax.ShapeDtypeStruct(adj_source.shape, f32),
            jax.ShapeDtypeStruct((blocks, size), f32),
        ),
        in_specs=[hbm] * 7,
        out_specs=(hbm,) * 3,
        scratch_shapes=[
            pltpu.SMEM((links, blocks), jnp.int32),
            pltpu.SMEM((rounds, tiles), jnp.int32),
            pltpu.SMEM((count,), f32),
            pltpu.VMEM(fwd_source.shape, f32),
            pltpu.VMEM(adj_source.shape, f32),
            pltpu.VMEM((blocks, size), f32),
            pltpu.VMEM(curl_blocks.shape, f32),
            pltpu.VMEM((blocks, links * size, 2 * size), bf16),
            pltpu.VMEM((blocks, width // 2, size), f32),
            pltpu.VMEM((blocks, width, size), f32),
            pltpu.VMEM((blocks, width, size), f32),
            pltpu.VMEM((blocks, width, size), f32),
            pltpu.VMEM((blocks, width, size), f32),
            pltpu.VMEM((blocks + sent, width, size), f32),
            pltpu.VMEM((blocks + sent, width, size), f32),
            pltpu.VMEM((sent, width, size), f32),
            pltpu.VMEM((sent, width, size), f32),
            pltpu.VMEM((peers, blocks, size), f32),
            pltpu.SemaphoreType.DMA((9,)),
            pltpu.SemaphoreType.DMA((blocks // CHUNK,)),
            pltpu.SemaphoreType.DMA((2, rounds, 2)),
            pltpu.SemaphoreType.DMA((2, rounds, 2)),
            pltpu.SemaphoreType.DMA((peers,)),
            pltpu.SemaphoreType.DMA((peers,)),
        ],
        compiler_params=pltpu.CompilerParams(
            collective_id=0, has_side_effects=True, vmem_limit_bytes=VMEM
        ),
    )(
        block_links.T,
        tile_lists,
        omega,
        fwd_source,
        adj_source,
        curl_blocks,
        edge_mass,
    )
    scale = 1.0 / (24.0 * count * peers) ** 0.5
    fwd_field, adj_field, model = pl.pallas_call(
        functools.partial(finish, scale),
        out_shape=(
            jax.ShapeDtypeStruct(fwd_source.shape, f32),
            jax.ShapeDtypeStruct(adj_source.shape, f32),
            jax.ShapeDtypeStruct(cond.shape, f32),
        ),
        in_specs=[hbm] * 5,
        out_specs=(hbm, hbm, vmem),
        scratch_shapes=[
            pltpu.VMEM((blocks, size), f32),
            pltpu.VMEM(cell_edges.shape, jnp.int32),
            pltpu.VMEM(cond.shape, f32),
            pltpu.VMEM(fwd_source.shape, f32),
            pltpu.VMEM(adj_source.shape, f32),
            pltpu.SemaphoreType.DMA((7,)),
        ],
        compiler_params=pltpu.CompilerParams(vmem_limit_bytes=VMEM),
    )(fields, adjoint, edge, cell_edges, cond)
    return fwd_field, adj_field, model.reshape(cells)


def solution(mesh):
    in_specs = (
        P("freq", None, "dom", None),
        P("freq", None, "dom", None),
        P("dom", None, None, None),
        P("dom", None),
        P("dom", None),
        P("dom", None),
        P("freq"),
        P(None, "dom"),
        P("dom"),
    )
    out_specs = (P("freq", None, "dom", None), P("freq", None, "dom", None), P("dom"))
    return jax.shard_map(local, mesh=mesh, in_specs=in_specs, out_specs=out_specs, check_vma=False)
```

```python
import functools

import jax
import jax.numpy as jnp
from jax import lax
from jax.experimental import pallas as pl
from jax.experimental.pallas import tpu as pltpu
from jax.sharding import PartitionSpec as P

THETA = 1.0
DELTA = 0.7
MESH = pl.DeviceIdType.MESH
VMEM = 63 * 1024 * 1024
CHUNK = 4
UNROLL = 8


def chebyshev_factors():
    sone = THETA / DELTA
    rho = 1.0 / sone
    factors = []
    for _ in range(2):
        rho_new = 1.0 / (2.0 * sone - rho)
        factors.append((rho_new * rho, 2.0 * rho_new / DELTA))
        rho = rho_new
    return factors


def split(value):
    high = value.astype(jnp.bfloat16)
    low = (value - high.astype(jnp.float32)).astype(jnp.bfloat16)
    return high, low


def row_of(count, system, f, c):
    return (c % 2) * 4 * count + system * 2 * count + f * 2 + c // 2


def kernel(
    peers,
    links_hbm,
    tiles_hbm,
    omega_hbm,
    fwd_hbm,
    adj_hbm,
    curl_hbm,
    mass_hbm,
    fwd_out,
    adj_out,
    edge_out,
    links_ref,
    tiles_ref,
    omega_ref,
    fwd_ref,
    adj_ref,
    mass_ref,
    raw,
    parts,
    weight,
    first,
    second,
    resid,
    total,
    ext_one,
    ext_two,
    send_one,
    send_two,
    terms,
    load_sem,
    raw_sem,
    send_sem,
    recv_sem,
    term_send_sem,
    term_recv_sem,
):
    blocks, size = mass_ref.shape
    count = fwd_ref.shape[0]
    width = 8 * count
    half = width // 2
    rounds, tiles = tiles_ref.shape
    links = links_ref.shape[0]
    freq = lax.axis_index("freq")
    dom = lax.axis_index("dom")

    loads = {}
    for at, (name, source, target) in enumerate(
        (
            ("fwd", fwd_hbm, fwd_ref),
            ("adj", adj_hbm, adj_ref),
            ("tiles", tiles_hbm, tiles_ref),
            ("links", links_hbm, links_ref),
            ("omega", omega_hbm, omega_ref),
            ("mass", mass_hbm, mass_ref),
        )
    ):
        loads[name] = pltpu.make_async_copy(source, target, load_sem.at[at])
        loads[name].start()

    def raw_copy(chunk):
        rows = pl.ds(chunk * CHUNK, CHUNK)
        return pltpu.make_async_copy(curl_hbm.at[rows], raw.at[rows], raw_sem.at[chunk])

    for chunk in range(blocks // CHUNK):
        raw_copy(chunk).start()

    partners = []
    for bit in range(rounds):
        mask = 2**bit
        partners.append((freq, dom + mask * (1 - 2 * ((dom // mask) % 2))))
    others = [(lax.rem(freq + step, peers), dom) for step in range(1, peers)]

    barrier = pltpu.get_barrier_semaphore()
    for device in partners + others:
        pl.semaphore_signal(barrier, inc=1, device_id=device, device_id_type=MESH)

    for system, (name, ref) in enumerate((("fwd", fwd_ref), ("adj", adj_ref))):
        loads[name].wait()
        for f in range(count):
            for c in range(4):
                first[:, row_of(count, system, f, c), :] = ref[f, c]

    pieces = 2
    span = tiles // pieces

    def push(send, ext, phase, bit, piece):
        rows = bit * tiles + piece * span
        copy = pltpu.make_async_remote_copy(
            src_ref=send.at[pl.ds(rows, span)],
            dst_ref=ext.at[pl.ds(blocks + rows, span)],
            send_sem=send_sem.at[phase, bit, piece],
            recv_sem=recv_sem.at[phase, bit, piece],
            device_id=partners[bit],
            device_id_type=MESH,
        )
        copy.start()
        return copy

    loads["tiles"].wait()
    copies = []
    for bit in reversed(range(rounds)):
        for piece in range(pieces):
            for tile in range(piece * span, (piece + 1) * span):
                send_one[bit * tiles + tile] = first[tiles_ref[bit, tile]]
            if len(copies) == 0:
                pl.semaphore_wait(barrier, len(partners) + len(others))
            copies.append(push(send_one, ext_one, 0, bit, piece))
    ext_one[pl.ds(0, blocks)] = first[...]

    for name in ("links", "omega", "mass"):
        loads[name].wait()
    place = lax.broadcasted_iota(jnp.int32, (half, size), 0)
    place = lax.rem(place // 2, count)
    omega = jnp.zeros((half, size), jnp.float32)
    for f in range(count):
        omega = jnp.where(place == f, omega_ref[f], omega)
    for row in range(blocks):
        weight[row] = omega * mass_ref[pl.ds(row, 1), :]

    for chunk in range(blocks // CHUNK):
        raw_copy(chunk).wait()

        def cut(step, carry):
            row = chunk * CHUNK + step
            for link in range(links):
                high, low = split(raw[row, link].T)
                rows = pl.ds(link * size, size)
                parts[row, rows, pl.ds(0, size)] = high
                parts[row, rows, pl.ds(size, size)] = low
            return carry

        lax.fori_loop(0, CHUNK, cut, 0)

    def operate(row, field, ext):
        gathered = [ext[links_ref[link, row]] for link in range(links)]
        high, low = split(jnp.concatenate(gathered, axis=1))
        both = jnp.concatenate([high, low], axis=0)
        product = jnp.dot(both, parts[row], preferred_element_type=jnp.float32)
        product = product[:width] + product[width:]
        curl = product[:, :size] + product[:, size:]
        value = field[row]
        turned = jnp.concatenate([-value[half:], value[:half]], axis=0)
        scale = weight[row]
        return value, curl + jnp.concatenate([scale, scale], axis=0) * turned

    factors = chebyshev_factors()

    def advance(row):
        keep, gain = factors[0]
        value, image = operate(row, first, ext_one)
        left = value - image
        return left, keep * value + gain * left

    for copy in copies:
        copy.wait()

    copies = []
    for bit in reversed(range(rounds)[-1:]):
        for piece in range(pieces):

            def ahead(step, carry):
                for inner in range(UNROLL):
                    tile = piece * span + step * UNROLL + inner
                    send_two[bit * tiles + tile] = advance(tiles_ref[bit, tile])[1]
                return carry

            lax.fori_loop(0, span // UNROLL, ahead, 0)
            copies.append(push(send_two, ext_two, 1, bit, piece))

    def one(step, carry):
        for inner in range(UNROLL):
            row = step * UNROLL + inner
            left, value = advance(row)
            resid[row] = left
            second[row] = value
        return carry

    lax.fori_loop(0, blocks // UNROLL, one, 0)
    for bit in reversed(range(rounds)[:-1]):
        for piece in range(pieces):
            for tile in range(piece * span, (piece + 1) * span):
                send_two[bit * tiles + tile] = second[tiles_ref[bit, tile]]
            copies.append(push(send_two, ext_two, 1, bit, piece))
    ext_two[pl.ds(0, blocks)] = second[...]
    for copy in copies:
        copy.wait()

    def two(step, carry):
        keep, gain = factors[1]
        for inner in range(UNROLL):
            row = step * UNROLL + inner
            value, image = operate(row, second, ext_two)
            left = resid[row] - image
            done = (first[row] + value) + (keep * value + gain * left)
            total[row] = done
            crossed = jnp.concatenate([done[half + half // 2 :], done[half : half + half // 2]], axis=0)
            term = omega * done[:half] * crossed
            terms[freq, pl.ds(row, 1), :] = jnp.sum(term, axis=0, keepdims=True)
        return carry

    lax.fori_loop(0, blocks // UNROLL, two, 0)

    copies = []
    for step in range(1, peers):
        copy = pltpu.make_async_remote_copy(
            src_ref=terms.at[freq],
            dst_ref=terms.at[freq],
            send_sem=term_send_sem.at[step],
            recv_sem=term_recv_sem.at[step],
            device_id=others[step - 1],
            device_id_type=MESH,
        )
        copy.start()
        copies.append(copy)
    for system, ref in enumerate((fwd_ref, adj_ref)):
        for f in range(count):
            for c in range(4):
                ref[f, c] = total[:, row_of(count, system, f, c), :]
    stores = []
    for at, (source, target) in enumerate(((fwd_ref, fwd_out), (adj_ref, adj_out))):
        stores.append(pltpu.make_async_copy(source, target, load_sem.at[6 + at]))
        stores[-1].start()
    for copy in copies:
        copy.wait()
    whole = terms[0]
    for peer in range(1, peers):
        whole = whole + terms[peer]
    mass_ref[...] = whole
    stores.append(pltpu.make_async_copy(mass_ref, edge_out, load_sem.at[8]))
    stores[-1].start()
    for copy in stores:
        copy.wait()


def finish(
    scale,
    fwd_hbm,
    adj_hbm,
    edge_hbm,
    cells_hbm,
    cond_hbm,
    fwd_out,
    adj_out,
    model_out,
    edge_ref,
    cells_ref,
    cond_ref,
    fwd_ref,
    adj_ref,
    copy_sem,
):
    pairs = (
        (edge_hbm, edge_ref),
        (cells_hbm, cells_ref),
        (cond_hbm, cond_ref),
        (fwd_hbm, fwd_ref),
        (adj_hbm, adj_ref),
        (fwd_ref, fwd_out),
        (adj_ref, adj_out),
    )
    copies = [pltpu.make_async_copy(*pair, copy_sem.at[at]) for at, pair in enumerate(pairs)]
    for copy in copies[:5]:
        copy.start()
    for copy in copies[:5]:
        copy.wait()
    for copy in copies[5:]:
        copy.start()

    blocks, size = edge_ref.shape
    corners, cells = cells_ref.shape
    shift = size.bit_length() - 1
    sums = []
    for column in range(cells // size):
        acc = jnp.zeros((1, size), jnp.float32)
        for start in range(0, corners, 8):
            rows = min(8, corners - start)
            ids = cells_ref[pl.ds(start, rows), pl.ds(column * size, size)]
            if rows < 8:
                ids = jnp.concatenate([ids, jnp.full((8 - rows, size), -1, jnp.int32)], axis=0)
            block = ids >> shift
            lane = ids & (size - 1)
            found = jnp.zeros((8, size), jnp.float32)
            for row in range(blocks):
                values = jnp.broadcast_to(edge_ref[pl.ds(row, 1), :], (8, size))
                got = jnp.take_along_axis(values, lane, axis=1, mode="promise_in_bounds")
                found = jnp.where(block == row, got, found)
            acc = acc + jnp.sum(found, axis=0, keepdims=True)
        sums.append(acc)
    grad = jnp.concatenate(sums, axis=0) * scale
    model_out[...] = cond_ref[...] - 0.5 * grad / jnp.sqrt(grad * grad + 1.0)
    for copy in copies[5:]:
        copy.wait()


def local(
    fwd_source,
    adj_source,
    curl_blocks,
    block_links,
    tile_lists,
    edge_mass,
    omega,
    cell_edges,
    log_cond,
):
    count, _, blocks, size = fwd_source.shape
    peers = lax.axis_size("freq")
    width = 8 * count
    rounds, tiles = tile_lists.shape
    sent = rounds * tiles
    links = block_links.shape[1]
    cells = log_cond.shape[0]
    cond = log_cond.reshape(cells // size, size)
    f32, bf16 = jnp.float32, jnp.bfloat16
    vmem = pl.BlockSpec(memory_space=pltpu.VMEM)
    hbm = pl.BlockSpec(memory_space=pltpu.HBM)
    fields, adjoint, edge = pl.pallas_call(
        functools.partial(kernel, peers),
        out_shape=(
            jax.ShapeDtypeStruct(fwd_source.shape, f32),
            jax.ShapeDtypeStruct(adj_source.shape, f32),
            jax.ShapeDtypeStruct((blocks, size), f32),
        ),
        in_specs=[hbm] * 7,
        out_specs=(hbm,) * 3,
        scratch_shapes=[
            pltpu.SMEM((links, blocks), jnp.int32),
            pltpu.SMEM((rounds, tiles), jnp.int32),
            pltpu.SMEM((count,), f32),
            pltpu.VMEM(fwd_source.shape, f32),
            pltpu.VMEM(adj_source.shape, f32),
            pltpu.VMEM((blocks, size), f32),
            pltpu.VMEM(curl_blocks.shape, f32),
            pltpu.VMEM((blocks, links * size, 2 * size), bf16),
            pltpu.VMEM((blocks, width // 2, size), f32),
            pltpu.VMEM((blocks, width, size), f32),
            pltpu.VMEM((blocks, width, size), f32),
            pltpu.VMEM((blocks, width, size), f32),
            pltpu.VMEM((blocks, width, size), f32),
            pltpu.VMEM((blocks + sent, width, size), f32),
            pltpu.VMEM((blocks + sent, width, size), f32),
            pltpu.VMEM((sent, width, size), f32),
            pltpu.VMEM((sent, width, size), f32),
            pltpu.VMEM((peers, blocks, size), f32),
            pltpu.SemaphoreType.DMA((9,)),
            pltpu.SemaphoreType.DMA((blocks // CHUNK,)),
            pltpu.SemaphoreType.DMA((2, rounds, 2)),
            pltpu.SemaphoreType.DMA((2, rounds, 2)),
            pltpu.SemaphoreType.DMA((peers,)),
            pltpu.SemaphoreType.DMA((peers,)),
        ],
        compiler_params=pltpu.CompilerParams(
            collective_id=0, has_side_effects=True, vmem_limit_bytes=VMEM
        ),
    )(
        block_links.T,
        tile_lists,
        omega,
        fwd_source,
        adj_source,
        curl_blocks,
        edge_mass,
    )
    scale = 1.0 / (24.0 * count * peers) ** 0.5
    fwd_field, adj_field, model = pl.pallas_call(
        functools.partial(finish, scale),
        out_shape=(
            jax.ShapeDtypeStruct(fwd_source.shape, f32),
            jax.ShapeDtypeStruct(adj_source.shape, f32),
            jax.ShapeDtypeStruct(cond.shape, f32),
        ),
        in_specs=[hbm] * 5,
        out_specs=(hbm, hbm, vmem),
        scratch_shapes=[
            pltpu.VMEM((blocks, size), f32),
            pltpu.VMEM(cell_edges.shape, jnp.int32),
            pltpu.VMEM(cond.shape, f32),
            pltpu.VMEM(fwd_source.shape, f32),
            pltpu.VMEM(adj_source.shape, f32),
            pltpu.SemaphoreType.DMA((7,)),
        ],
        compiler_params=pltpu.CompilerParams(vmem_limit_bytes=VMEM),
    )(fields, adjoint, edge, cell_edges, cond)
    return fwd_field, adj_field, model.reshape(cells)


def solution(mesh):
    in_specs = (
        P("freq", None, "dom", None),
        P("freq", None, "dom", None),
        P("dom", None, None, None),
        P("dom", None),
        P("dom", None),
        P("dom", None),
        P("freq"),
        P(None, "dom"),
        P("dom"),
    )
    out_specs = (P("freq", None, "dom", None), P("freq", None, "dom", None), P("dom"))
    return jax.shard_map(local, mesh=mesh, in_specs=in_specs, out_specs=out_specs, check_vma=False)
```

```python
import functools

import jax
import jax.numpy as jnp
from jax import lax
from jax.experimental import pallas as pl
from jax.experimental.pallas import tpu as pltpu
from jax.sharding import PartitionSpec as P

THETA = 1.0
DELTA = 0.7
MESH = pl.DeviceIdType.MESH
VMEM = 63 * 1024 * 1024
CHUNK = 4
UNROLL = 8


def chebyshev_factors():
    sone = THETA / DELTA
    rho = 1.0 / sone
    factors = []
    for _ in range(2):
        rho_new = 1.0 / (2.0 * sone - rho)
        factors.append((rho_new * rho, 2.0 * rho_new / DELTA))
        rho = rho_new
    return factors


def split(value):
    high = value.astype(jnp.bfloat16)
    low = (value - high.astype(jnp.float32)).astype(jnp.bfloat16)
    return high, low


def row_of(count, system, f, c):
    return (c % 2) * 4 * count + system * 2 * count + f * 2 + c // 2


def kernel(
    peers,
    links_hbm,
    tiles_hbm,
    omega_hbm,
    fwd_hbm,
    adj_hbm,
    curl_hbm,
    mass_hbm,
    fwd_out,
    adj_out,
    edge_out,
    links_ref,
    tiles_ref,
    omega_ref,
    fwd_ref,
    adj_ref,
    mass_ref,
    raw,
    parts,
    weight,
    first,
    second,
    resid,
    total,
    ext_one,
    ext_two,
    send_one,
    send_two,
    terms,
    load_sem,
    raw_sem,
    send_sem,
    recv_sem,
    term_send_sem,
    term_recv_sem,
):
    blocks, size = mass_ref.shape
    count = fwd_ref.shape[0]
    width = 8 * count
    half = width // 2
    rounds, tiles = tiles_ref.shape
    links = links_ref.shape[0]
    freq = lax.axis_index("freq")
    dom = lax.axis_index("dom")

    loads = {}
    for at, (name, source, target) in enumerate(
        (
            ("fwd", fwd_hbm, fwd_ref),
            ("adj", adj_hbm, adj_ref),
            ("tiles", tiles_hbm, tiles_ref),
            ("links", links_hbm, links_ref),
            ("omega", omega_hbm, omega_ref),
            ("mass", mass_hbm, mass_ref),
        )
    ):
        loads[name] = pltpu.make_async_copy(source, target, load_sem.at[at])
        loads[name].start()

    def raw_copy(chunk):
        rows = pl.ds(chunk * CHUNK, CHUNK)
        return pltpu.make_async_copy(curl_hbm.at[rows], raw.at[rows], raw_sem.at[chunk])

    for chunk in range(blocks // CHUNK):
        raw_copy(chunk).start()

    partners = []
    for bit in range(rounds):
        mask = 2**bit
        partners.append((freq, dom + mask * (1 - 2 * ((dom // mask) % 2))))
    others = [(lax.rem(freq + step, peers), dom) for step in range(1, peers)]

    barrier = pltpu.get_barrier_semaphore()
    for device in partners + others:
        pl.semaphore_signal(barrier, inc=1, device_id=device, device_id_type=MESH)

    for system, (name, ref) in enumerate((("fwd", fwd_ref), ("adj", adj_ref))):
        loads[name].wait()
        for f in range(count):
            for c in range(4):
                first[:, row_of(count, system, f, c), :] = ref[f, c]

    pieces = 2
    span = tiles // pieces

    def push(send, ext, phase, bit, piece):
        rows = bit * tiles + piece * span
        copy = pltpu.make_async_remote_copy(
            src_ref=send.at[pl.ds(rows, span)],
            dst_ref=ext.at[pl.ds(blocks + rows, span)],
            send_sem=send_sem.at[phase, bit, piece],
            recv_sem=recv_sem.at[phase, bit, piece],
            device_id=partners[bit],
            device_id_type=MESH,
        )
        copy.start()
        return copy

    loads["tiles"].wait()
    copies = []
    for bit in reversed(range(rounds)):
        for piece in range(pieces):
            for tile in range(piece * span, (piece + 1) * span):
                send_one[bit * tiles + tile] = first[tiles_ref[bit, tile]]
            if len(copies) == 0:
                pl.semaphore_wait(barrier, len(partners) + len(others))
            copies.append(push(send_one, ext_one, 0, bit, piece))
    ext_one[pl.ds(0, blocks)] = first[...]

    for name in ("links", "omega", "mass"):
        loads[name].wait()
    place = lax.broadcasted_iota(jnp.int32, (half, size), 0)
    place = lax.rem(place // 2, count)
    omega = jnp.zeros((half, size), jnp.float32)
    for f in range(count):
        omega = jnp.where(place == f, omega_ref[f], omega)
    for row in range(blocks):
        weight[row] = omega * mass_ref[pl.ds(row, 1), :]

    for chunk in range(blocks // CHUNK):
        raw_copy(chunk).wait()

        def cut(step, carry):
            row = chunk * CHUNK + step
            for link in range(links):
                high, low = split(raw[row, link])
                columns = pl.ds(link * size, size)
                parts[row, pl.ds(0, size), columns] = high
                parts[row, pl.ds(size, size), columns] = low
            return carry

        lax.fori_loop(0, CHUNK, cut, 0)

    def operate(row, field, ext):
        gathered = [ext[links_ref[link, row]] for link in range(links)]
        high, low = split(jnp.concatenate(gathered, axis=1))
        both = jnp.concatenate([high, low], axis=0)
        product = lax.dot_general(
            parts[row], both, (((1,), (1,)), ((), ())), preferred_element_type=jnp.float32
        )
        product = (product[:size] + product[size:]).T
        curl = product[:width] + product[width:]
        value = field[row]
        turned = jnp.concatenate([-value[half:], value[:half]], axis=0)
        scale = weight[row]
        return value, curl + jnp.concatenate([scale, scale], axis=0) * turned

    factors = chebyshev_factors()

    def advance(row):
        keep, gain = factors[0]
        value, image = operate(row, first, ext_one)
        left = value - image
        return left, keep * value + gain * left

    for copy in copies:
        copy.wait()

    copies = []
    for bit in reversed(range(rounds)[-1:]):
        for piece in range(pieces):

            def ahead(step, carry):
                for inner in range(UNROLL):
                    tile = piece * span + step * UNROLL + inner
                    send_two[bit * tiles + tile] = advance(tiles_ref[bit, tile])[1]
                return carry

            lax.fori_loop(0, span // UNROLL, ahead, 0)
            copies.append(push(send_two, ext_two, 1, bit, piece))

    def one(step, carry):
        for inner in range(UNROLL):
            row = step * UNROLL + inner
            left, value = advance(row)
            resid[row] = left
            second[row] = value
        return carry

    lax.fori_loop(0, blocks // UNROLL, one, 0)
    for bit in reversed(range(rounds)[:-1]):
        for piece in range(pieces):
            for tile in range(piece * span, (piece + 1) * span):
                send_two[bit * tiles + tile] = second[tiles_ref[bit, tile]]
            copies.append(push(send_two, ext_two, 1, bit, piece))
    ext_two[pl.ds(0, blocks)] = second[...]
    for copy in copies:
        copy.wait()

    def two(step, carry):
        keep, gain = factors[1]
        for inner in range(UNROLL):
            row = step * UNROLL + inner
            value, image = operate(row, second, ext_two)
            left = resid[row] - image
            done = (first[row] + value) + (keep * value + gain * left)
            total[row] = done
            crossed = jnp.concatenate([done[half + half // 2 :], done[half : half + half // 2]], axis=0)
            term = omega * done[:half] * crossed
            terms[freq, pl.ds(row, 1), :] = jnp.sum(term, axis=0, keepdims=True)
        return carry

    lax.fori_loop(0, blocks // UNROLL, two, 0)

    copies = []
    for step in range(1, peers):
        copy = pltpu.make_async_remote_copy(
            src_ref=terms.at[freq],
            dst_ref=terms.at[freq],
            send_sem=term_send_sem.at[step],
            recv_sem=term_recv_sem.at[step],
            device_id=others[step - 1],
            device_id_type=MESH,
        )
        copy.start()
        copies.append(copy)
    for system, ref in enumerate((fwd_ref, adj_ref)):
        for f in range(count):
            for c in range(4):
                ref[f, c] = total[:, row_of(count, system, f, c), :]
    stores = []
    for at, (source, target) in enumerate(((fwd_ref, fwd_out), (adj_ref, adj_out))):
        stores.append(pltpu.make_async_copy(source, target, load_sem.at[6 + at]))
        stores[-1].start()
    for copy in copies:
        copy.wait()
    whole = terms[0]
    for peer in range(1, peers):
        whole = whole + terms[peer]
    mass_ref[...] = whole
    stores.append(pltpu.make_async_copy(mass_ref, edge_out, load_sem.at[8]))
    stores[-1].start()
    for copy in stores:
        copy.wait()


def finish(
    scale,
    fwd_hbm,
    adj_hbm,
    edge_hbm,
    cells_hbm,
    cond_hbm,
    fwd_out,
    adj_out,
    model_out,
    edge_ref,
    cells_ref,
    cond_ref,
    fwd_ref,
    adj_ref,
    copy_sem,
):
    pairs = (
        (edge_hbm, edge_ref),
        (cells_hbm, cells_ref),
        (cond_hbm, cond_ref),
        (fwd_hbm, fwd_ref),
        (adj_hbm, adj_ref),
        (fwd_ref, fwd_out),
        (adj_ref, adj_out),
    )
    copies = [pltpu.make_async_copy(*pair, copy_sem.at[at]) for at, pair in enumerate(pairs)]
    for copy in copies[:5]:
        copy.start()
    for copy in copies[:5]:
        copy.wait()
    for copy in copies[5:]:
        copy.start()

    blocks, size = edge_ref.shape
    corners, cells = cells_ref.shape
    shift = size.bit_length() - 1
    sums = []
    for column in range(cells // size):
        acc = jnp.zeros((1, size), jnp.float32)
        for start in range(0, corners, 8):
            rows = min(8, corners - start)
            ids = cells_ref[pl.ds(start, rows), pl.ds(column * size, size)]
            if rows < 8:
                ids = jnp.concatenate([ids, jnp.full((8 - rows, size), -1, jnp.int32)], axis=0)
            block = ids >> shift
            lane = ids & (size - 1)
            found = jnp.zeros((8, size), jnp.float32)
            for row in range(blocks):
                values = jnp.broadcast_to(edge_ref[pl.ds(row, 1), :], (8, size))
                got = jnp.take_along_axis(values, lane, axis=1, mode="promise_in_bounds")
                found = jnp.where(block == row, got, found)
            acc = acc + jnp.sum(found, axis=0, keepdims=True)
        sums.append(acc)
    grad = jnp.concatenate(sums, axis=0) * scale
    model_out[...] = cond_ref[...] - 0.5 * grad / jnp.sqrt(grad * grad + 1.0)
    for copy in copies[5:]:
        copy.wait()


def local(
    fwd_source,
    adj_source,
    curl_blocks,
    block_links,
    tile_lists,
    edge_mass,
    omega,
    cell_edges,
    log_cond,
):
    count, _, blocks, size = fwd_source.shape
    peers = lax.axis_size("freq")
    width = 8 * count
    rounds, tiles = tile_lists.shape
    sent = rounds * tiles
    links = block_links.shape[1]
    cells = log_cond.shape[0]
    cond = log_cond.reshape(cells // size, size)
    f32, bf16 = jnp.float32, jnp.bfloat16
    vmem = pl.BlockSpec(memory_space=pltpu.VMEM)
    hbm = pl.BlockSpec(memory_space=pltpu.HBM)
    fields, adjoint, edge = pl.pallas_call(
        functools.partial(kernel, peers),
        out_shape=(
            jax.ShapeDtypeStruct(fwd_source.shape, f32),
            jax.ShapeDtypeStruct(adj_source.shape, f32),
            jax.ShapeDtypeStruct((blocks, size), f32),
        ),
        in_specs=[hbm] * 7,
        out_specs=(hbm,) * 3,
        scratch_shapes=[
            pltpu.SMEM((links, blocks), jnp.int32),
            pltpu.SMEM((rounds, tiles), jnp.int32),
            pltpu.SMEM((count,), f32),
            pltpu.VMEM(fwd_source.shape, f32),
            pltpu.VMEM(adj_source.shape, f32),
            pltpu.VMEM((blocks, size), f32),
            pltpu.VMEM(curl_blocks.shape, f32),
            pltpu.VMEM((blocks, 2 * size, links * size), bf16),
            pltpu.VMEM((blocks, width // 2, size), f32),
            pltpu.VMEM((blocks, width, size), f32),
            pltpu.VMEM((blocks, width, size), f32),
            pltpu.VMEM((blocks, width, size), f32),
            pltpu.VMEM((blocks, width, size), f32),
            pltpu.VMEM((blocks + sent, width, size), f32),
            pltpu.VMEM((blocks + sent, width, size), f32),
            pltpu.VMEM((sent, width, size), f32),
            pltpu.VMEM((sent, width, size), f32),
            pltpu.VMEM((peers, blocks, size), f32),
            pltpu.SemaphoreType.DMA((9,)),
            pltpu.SemaphoreType.DMA((blocks // CHUNK,)),
            pltpu.SemaphoreType.DMA((2, rounds, 2)),
            pltpu.SemaphoreType.DMA((2, rounds, 2)),
            pltpu.SemaphoreType.DMA((peers,)),
            pltpu.SemaphoreType.DMA((peers,)),
        ],
        compiler_params=pltpu.CompilerParams(
            collective_id=0, has_side_effects=True, vmem_limit_bytes=VMEM
        ),
    )(
        block_links.T,
        tile_lists,
        omega,
        fwd_source,
        adj_source,
        curl_blocks,
        edge_mass,
    )
    scale = 1.0 / (24.0 * count * peers) ** 0.5
    fwd_field, adj_field, model = pl.pallas_call(
        functools.partial(finish, scale),
        out_shape=(
            jax.ShapeDtypeStruct(fwd_source.shape, f32),
            jax.ShapeDtypeStruct(adj_source.shape, f32),
            jax.ShapeDtypeStruct(cond.shape, f32),
        ),
        in_specs=[hbm] * 5,
        out_specs=(hbm, hbm, vmem),
        scratch_shapes=[
            pltpu.VMEM((blocks, size), f32),
            pltpu.VMEM(cell_edges.shape, jnp.int32),
            pltpu.VMEM(cond.shape, f32),
            pltpu.VMEM(fwd_source.shape, f32),
            pltpu.VMEM(adj_source.shape, f32),
            pltpu.SemaphoreType.DMA((7,)),
        ],
        compiler_params=pltpu.CompilerParams(vmem_limit_bytes=VMEM),
    )(fields, adjoint, edge, cell_edges, cond)
    return fwd_field, adj_field, model.reshape(cells)


def solution(mesh):
    in_specs = (
        P("freq", None, "dom", None),
        P("freq", None, "dom", None),
        P("dom", None, None, None),
        P("dom", None),
        P("dom", None),
        P("dom", None),
        P("freq"),
        P(None, "dom"),
        P("dom"),
    )
    out_specs = (P("freq", None, "dom", None), P("freq", None, "dom", None), P("dom"))
    return jax.shard_map(local, mesh=mesh, in_specs=in_specs, out_specs=out_specs, check_vma=False)
```

```python
import functools

import jax
import jax.numpy as jnp
from jax import lax
from jax.experimental import pallas as pl
from jax.experimental.pallas import tpu as pltpu
from jax.sharding import PartitionSpec as P

THETA = 1.0
DELTA = 0.7
MESH = pl.DeviceIdType.MESH
VMEM = 63 * 1024 * 1024
CHUNK = 4
UNROLL = 8


def chebyshev_factors():
    sone = THETA / DELTA
    rho = 1.0 / sone
    factors = []
    for _ in range(2):
        rho_new = 1.0 / (2.0 * sone - rho)
        factors.append((rho_new * rho, 2.0 * rho_new / DELTA))
        rho = rho_new
    return factors


def split(value):
    high = value.astype(jnp.bfloat16)
    low = (value - high.astype(jnp.float32)).astype(jnp.bfloat16)
    return high, low


def row_of(count, system, f, c):
    return (c % 2) * 4 * count + system * 2 * count + f * 2 + c // 2


def kernel(
    peers,
    links_hbm,
    tiles_hbm,
    omega_hbm,
    fwd_hbm,
    adj_hbm,
    curl_hbm,
    mass_hbm,
    fwd_out,
    adj_out,
    edge_out,
    links_ref,
    tiles_ref,
    omega_ref,
    fwd_ref,
    adj_ref,
    mass_ref,
    raw,
    parts_own,
    parts,
    near,
    weight,
    first,
    second,
    resid,
    total,
    ext_one,
    ext_two,
    send_one,
    send_two,
    terms,
    load_sem,
    raw_sem,
    send_sem,
    recv_sem,
    term_send_sem,
    term_recv_sem,
):
    blocks, size = mass_ref.shape
    count = fwd_ref.shape[0]
    width = 8 * count
    half = width // 2
    rounds, tiles = tiles_ref.shape
    links = links_ref.shape[0]
    freq = lax.axis_index("freq")
    dom = lax.axis_index("dom")

    loads = {}
    for at, (name, source, target) in enumerate(
        (
            ("fwd", fwd_hbm, fwd_ref),
            ("adj", adj_hbm, adj_ref),
            ("tiles", tiles_hbm, tiles_ref),
            ("links", links_hbm, links_ref),
            ("omega", omega_hbm, omega_ref),
            ("mass", mass_hbm, mass_ref),
        )
    ):
        loads[name] = pltpu.make_async_copy(source, target, load_sem.at[at])
        loads[name].start()

    def raw_copy(chunk):
        rows = pl.ds(chunk * CHUNK, CHUNK)
        return pltpu.make_async_copy(curl_hbm.at[rows], raw.at[rows], raw_sem.at[chunk])

    for chunk in range(blocks // CHUNK):
        raw_copy(chunk).start()

    partners = []
    for bit in range(rounds):
        mask = 2**bit
        partners.append((freq, dom + mask * (1 - 2 * ((dom // mask) % 2))))
    others = [(lax.rem(freq + step, peers), dom) for step in range(1, peers)]

    barrier = pltpu.get_barrier_semaphore()
    for device in partners + others:
        pl.semaphore_signal(barrier, inc=1, device_id=device, device_id_type=MESH)

    for system, (name, ref) in enumerate((("fwd", fwd_ref), ("adj", adj_ref))):
        loads[name].wait()
        for f in range(count):
            for c in range(4):
                first[:, row_of(count, system, f, c), :] = ref[f, c]

    pieces = 2
    span = tiles // pieces

    def push(send, ext, phase, bit, piece):
        rows = bit * tiles + piece * span
        copy = pltpu.make_async_remote_copy(
            src_ref=send.at[pl.ds(rows, span)],
            dst_ref=ext.at[pl.ds(blocks + rows, span)],
            send_sem=send_sem.at[phase, bit, piece],
            recv_sem=recv_sem.at[phase, bit, piece],
            device_id=partners[bit],
            device_id_type=MESH,
        )
        copy.start()
        return copy

    loads["tiles"].wait()
    copies = []
    for bit in reversed(range(rounds)):
        for piece in range(pieces):
            for tile in range(piece * span, (piece + 1) * span):
                send_one[bit * tiles + tile] = first[tiles_ref[bit, tile]]
            if len(copies) == 0:
                pl.semaphore_wait(barrier, len(partners) + len(others))
            copies.append(push(send_one, ext_one, 0, bit, piece))
    ext_one[pl.ds(0, blocks)] = first[...]

    for name in ("links", "omega", "mass"):
        loads[name].wait()
    place = lax.broadcasted_iota(jnp.int32, (half, size), 0)
    place = lax.rem(place // 2, count)
    omega = jnp.zeros((half, size), jnp.float32)
    for f in range(count):
        omega = jnp.where(place == f, omega_ref[f], omega)
    for row in range(blocks):
        weight[row] = omega * mass_ref[pl.ds(row, 1), :]

    for chunk in range(blocks // CHUNK):
        raw_copy(chunk).wait()

        def cut(step, carry):
            row = chunk * CHUNK + step
            for link in range(links):
                high, low = split(raw[row, link].T)
                if link == 0:
                    parts_own[row, :, pl.ds(0, size)] = high
                    parts_own[row, :, pl.ds(size, size)] = low
                else:
                    rows = pl.ds((link - 1) * size, size)
                    parts[row, rows, pl.ds(0, size)] = high
                    parts[row, rows, pl.ds(size, size)] = low
            return carry

        lax.fori_loop(0, CHUNK, cut, 0)

    def stacked(value):
        return jnp.concatenate(split(value), axis=0)

    def folded(product):
        product = product[:width] + product[width:]
        return product[:, :size] + product[:, size:]

    def times(left, right):
        return jnp.dot(left, right, preferred_element_type=jnp.float32)

    def paired(one_left, two_left, one_right, two_right):
        blank = jnp.zeros_like(one_left)
        upper = jnp.concatenate([one_left, blank], axis=1)
        lower = jnp.concatenate([blank, two_left], axis=1)
        product = times(
            jnp.concatenate([upper, lower], axis=0),
            jnp.concatenate([one_right, two_right], axis=0),
        )
        return folded(product[: 2 * width]), folded(product[2 * width :])

    def own_blocks(field):
        def body(step, carry):
            for inner in range(0, UNROLL, 2):
                row = step * UNROLL + inner
                near[row], near[row + 1] = paired(
                    stacked(field[row]),
                    stacked(field[row + 1]),
                    parts_own[row],
                    parts_own[row + 1],
                )
            return carry

        lax.fori_loop(0, blocks // UNROLL, body, 0)

    def close(row, field, curl):
        value = field[row]
        turned = jnp.concatenate([-value[half:], value[:half]], axis=0)
        scale = weight[row]
        return value, curl + near[row] + jnp.concatenate([scale, scale], axis=0) * turned

    def operate(row, field, ext):
        gathered = [ext[links_ref[link, row]] for link in range(1, links)]
        left = stacked(jnp.concatenate(gathered, axis=1))
        return close(row, field, folded(times(left, parts[row])))

    def operate_two(row, field, ext):
        depth = (links - 2) * size
        curls = []
        for at in (row, row + 1):
            gathered = [ext[links_ref[link, at]] for link in range(1, links - 1)]
            left = stacked(jnp.concatenate(gathered, axis=1))
            curls.append(folded(times(left, parts[at, pl.ds(0, depth)])))
        last = paired(
            stacked(ext[links_ref[links - 1, row]]),
            stacked(ext[links_ref[links - 1, row + 1]]),
            parts[row, pl.ds(depth, size)],
            parts[row + 1, pl.ds(depth, size)],
        )
        return [
            close(at, field, curl + extra)
            for at, curl, extra in zip((row, row + 1), curls, last)
        ]

    factors = chebyshev_factors()

    def advance(value, image):
        keep, gain = factors[0]
        left = value - image
        return left, keep * value + gain * left

    own_blocks(first)
    for copy in copies:
        copy.wait()

    copies = []
    for bit in reversed(range(rounds)[-1:]):
        for piece in range(pieces):

            def ahead(step, carry):
                for inner in range(UNROLL):
                    tile = piece * span + step * UNROLL + inner
                    done = advance(*operate(tiles_ref[bit, tile], first, ext_one))
                    send_two[bit * tiles + tile] = done[1]
                return carry

            lax.fori_loop(0, span // UNROLL, ahead, 0)
            copies.append(push(send_two, ext_two, 1, bit, piece))

    def one(step, carry):
        for inner in range(0, UNROLL, 2):
            row = step * UNROLL + inner
            for at, pair in enumerate(operate_two(row, first, ext_one)):
                left, value = advance(*pair)
                resid[row + at] = left
                second[row + at] = value
        return carry

    lax.fori_loop(0, blocks // UNROLL, one, 0)
    for bit in reversed(range(rounds)[:-1]):
        for piece in range(pieces):
            for tile in range(piece * span, (piece + 1) * span):
                send_two[bit * tiles + tile] = second[tiles_ref[bit, tile]]
            copies.append(push(send_two, ext_two, 1, bit, piece))
    ext_two[pl.ds(0, blocks)] = second[...]
    own_blocks(second)
    for copy in copies:
        copy.wait()

    def two(step, carry):
        keep, gain = factors[1]
        for inner in range(0, UNROLL, 2):
            start = step * UNROLL + inner
            for at, (value, image) in enumerate(operate_two(start, second, ext_two)):
                row = start + at
                left = resid[row] - image
                done = (first[row] + value) + (keep * value + gain * left)
                total[row] = done
                crossed = jnp.concatenate(
                    [done[half + half // 2 :], done[half : half + half // 2]], axis=0
                )
                term = omega * done[:half] * crossed
                terms[freq, pl.ds(row, 1), :] = jnp.sum(term, axis=0, keepdims=True)
        return carry

    lax.fori_loop(0, blocks // UNROLL, two, 0)

    copies = []
    for step in range(1, peers):
        copy = pltpu.make_async_remote_copy(
            src_ref=terms.at[freq],
            dst_ref=terms.at[freq],
            send_sem=term_send_sem.at[step],
            recv_sem=term_recv_sem.at[step],
            device_id=others[step - 1],
            device_id_type=MESH,
        )
        copy.start()
        copies.append(copy)
    for system, ref in enumerate((fwd_ref, adj_ref)):
        for f in range(count):
            for c in range(4):
                ref[f, c] = total[:, row_of(count, system, f, c), :]
    stores = []
    for at, (source, target) in enumerate(((fwd_ref, fwd_out), (adj_ref, adj_out))):
        stores.append(pltpu.make_async_copy(source, target, load_sem.at[6 + at]))
        stores[-1].start()
    for copy in copies:
        copy.wait()
    whole = terms[0]
    for peer in range(1, peers):
        whole = whole + terms[peer]
    mass_ref[...] = whole
    stores.append(pltpu.make_async_copy(mass_ref, edge_out, load_sem.at[8]))
    stores[-1].start()
    for copy in stores:
        copy.wait()


def finish(
    scale,
    fwd_hbm,
    adj_hbm,
    edge_hbm,
    cells_hbm,
    cond_hbm,
    fwd_out,
    adj_out,
    model_out,
    edge_ref,
    cells_ref,
    cond_ref,
    fwd_ref,
    adj_ref,
    copy_sem,
):
    pairs = (
        (edge_hbm, edge_ref),
        (cells_hbm, cells_ref),
        (cond_hbm, cond_ref),
        (fwd_hbm, fwd_ref),
        (adj_hbm, adj_ref),
        (fwd_ref, fwd_out),
        (adj_ref, adj_out),
    )
    copies = [pltpu.make_async_copy(*pair, copy_sem.at[at]) for at, pair in enumerate(pairs)]
    for copy in copies[:5]:
        copy.start()
    for copy in copies[:5]:
        copy.wait()
    for copy in copies[5:]:
        copy.start()

    blocks, size = edge_ref.shape
    corners, cells = cells_ref.shape
    shift = size.bit_length() - 1
    sums = []
    for column in range(cells // size):
        acc = jnp.zeros((1, size), jnp.float32)
        for start in range(0, corners, 8):
            rows = min(8, corners - start)
            ids = cells_ref[pl.ds(start, rows), pl.ds(column * size, size)]
            if rows < 8:
                ids = jnp.concatenate([ids, jnp.full((8 - rows, size), -1, jnp.int32)], axis=0)
            block = ids >> shift
            lane = ids & (size - 1)
            found = jnp.zeros((8, size), jnp.float32)
            for row in range(blocks):
                values = jnp.broadcast_to(edge_ref[pl.ds(row, 1), :], (8, size))
                got = jnp.take_along_axis(values, lane, axis=1, mode="promise_in_bounds")
                found = jnp.where(block == row, got, found)
            acc = acc + jnp.sum(found, axis=0, keepdims=True)
        sums.append(acc)
    grad = jnp.concatenate(sums, axis=0) * scale
    model_out[...] = cond_ref[...] - 0.5 * grad / jnp.sqrt(grad * grad + 1.0)
    for copy in copies[5:]:
        copy.wait()


def local(
    fwd_source,
    adj_source,
    curl_blocks,
    block_links,
    tile_lists,
    edge_mass,
    omega,
    cell_edges,
    log_cond,
):
    count, _, blocks, size = fwd_source.shape
    peers = lax.axis_size("freq")
    width = 8 * count
    rounds, tiles = tile_lists.shape
    sent = rounds * tiles
    links = block_links.shape[1]
    cells = log_cond.shape[0]
    cond = log_cond.reshape(cells // size, size)
    f32, bf16 = jnp.float32, jnp.bfloat16
    vmem = pl.BlockSpec(memory_space=pltpu.VMEM)
    hbm = pl.BlockSpec(memory_space=pltpu.HBM)
    fields, adjoint, edge = pl.pallas_call(
        functools.partial(kernel, peers),
        out_shape=(
            jax.ShapeDtypeStruct(fwd_source.shape, f32),
            jax.ShapeDtypeStruct(adj_source.shape, f32),
            jax.ShapeDtypeStruct((blocks, size), f32),
        ),
        in_specs=[hbm] * 7,
        out_specs=(hbm,) * 3,
        scratch_shapes=[
            pltpu.SMEM((links, blocks), jnp.int32),
            pltpu.SMEM((rounds, tiles), jnp.int32),
            pltpu.SMEM((count,), f32),
            pltpu.VMEM(fwd_source.shape, f32),
            pltpu.VMEM(adj_source.shape, f32),
            pltpu.VMEM((blocks, size), f32),
            pltpu.VMEM(curl_blocks.shape, f32),
            pltpu.VMEM((blocks, size, 2 * size), bf16),
            pltpu.VMEM((blocks, (links - 1) * size, 2 * size), bf16),
            pltpu.VMEM((blocks, width, size), f32),
            pltpu.VMEM((blocks, width // 2, size), f32),
            pltpu.VMEM((blocks, width, size), f32),
            pltpu.VMEM((blocks, width, size), f32),
            pltpu.VMEM((blocks, width, size), f32),
            pltpu.VMEM((blocks, width, size), f32),
            pltpu.VMEM((blocks + sent, width, size), f32),
            pltpu.VMEM((blocks + sent, width, size), f32),
            pltpu.VMEM((sent, width, size), f32),
            pltpu.VMEM((sent, width, size), f32),
            pltpu.VMEM((peers, blocks, size), f32),
            pltpu.SemaphoreType.DMA((9,)),
            pltpu.SemaphoreType.DMA((blocks // CHUNK,)),
            pltpu.SemaphoreType.DMA((2, rounds, 2)),
            pltpu.SemaphoreType.DMA((2, rounds, 2)),
            pltpu.SemaphoreType.DMA((peers,)),
            pltpu.SemaphoreType.DMA((peers,)),
        ],
        compiler_params=pltpu.CompilerParams(
            collective_id=0, has_side_effects=True, vmem_limit_bytes=VMEM
        ),
    )(
        block_links.T,
        tile_lists,
        omega,
        fwd_source,
        adj_source,
        curl_blocks,
        edge_mass,
    )
    scale = 1.0 / (24.0 * count * peers) ** 0.5
    fwd_field, adj_field, model = pl.pallas_call(
        functools.partial(finish, scale),
        out_shape=(
            jax.ShapeDtypeStruct(fwd_source.shape, f32),
            jax.ShapeDtypeStruct(adj_source.shape, f32),
            jax.ShapeDtypeStruct(cond.shape, f32),
        ),
        in_specs=[hbm] * 5,
        out_specs=(hbm, hbm, vmem),
        scratch_shapes=[
            pltpu.VMEM((blocks, size), f32),
            pltpu.VMEM(cell_edges.shape, jnp.int32),
            pltpu.VMEM(cond.shape, f32),
            pltpu.VMEM(fwd_source.shape, f32),
            pltpu.VMEM(adj_source.shape, f32),
            pltpu.SemaphoreType.DMA((7,)),
        ],
        compiler_params=pltpu.CompilerParams(vmem_limit_bytes=VMEM),
    )(fields, adjoint, edge, cell_edges, cond)
    return fwd_field, adj_field, model.reshape(cells)


def solution(mesh):
    in_specs = (
        P("freq", None, "dom", None),
        P("freq", None, "dom", None),
        P("dom", None, None, None),
        P("dom", None),
        P("dom", None),
        P("dom", None),
        P("freq"),
        P(None, "dom"),
        P("dom"),
    )
    out_specs = (P("freq", None, "dom", None), P("freq", None, "dom", None), P("dom"))
    return jax.shard_map(local, mesh=mesh, in_specs=in_specs, out_specs=out_specs, check_vma=False)
```

```python
import functools

import jax
import jax.numpy as jnp
from jax import lax
from jax.experimental import pallas as pl
from jax.experimental.pallas import tpu as pltpu
from jax.sharding import PartitionSpec as P

THETA = 1.0
DELTA = 0.7
MESH = pl.DeviceIdType.MESH
VMEM = 63 * 1024 * 1024
CHUNK = 4
UNROLL = 16


def chebyshev_factors():
    sone = THETA / DELTA
    rho = 1.0 / sone
    factors = []
    for _ in range(2):
        rho_new = 1.0 / (2.0 * sone - rho)
        factors.append((rho_new * rho, 2.0 * rho_new / DELTA))
        rho = rho_new
    return factors


def split(value):
    high = value.astype(jnp.bfloat16)
    low = (value - high.astype(jnp.float32)).astype(jnp.bfloat16)
    return high, low


def row_of(count, system, f, c):
    return (c % 2) * 4 * count + system * 2 * count + f * 2 + c // 2


def kernel(
    peers,
    links_hbm,
    tiles_hbm,
    omega_hbm,
    fwd_hbm,
    adj_hbm,
    curl_hbm,
    mass_hbm,
    fwd_out,
    adj_out,
    edge_out,
    links_ref,
    tiles_ref,
    omega_ref,
    fwd_ref,
    adj_ref,
    mass_ref,
    raw,
    parts_own,
    parts,
    near,
    weight,
    first,
    second,
    resid,
    total,
    ext_one,
    ext_two,
    send_one,
    send_two,
    terms,
    load_sem,
    raw_sem,
    send_sem,
    recv_sem,
    term_send_sem,
    term_recv_sem,
):
    blocks, size = mass_ref.shape
    count = fwd_ref.shape[0]
    width = 8 * count
    half = width // 2
    rounds, tiles = tiles_ref.shape
    links = links_ref.shape[0]
    freq = lax.axis_index("freq")
    dom = lax.axis_index("dom")

    loads = {}
    for at, (name, source, target) in enumerate(
        (
            ("fwd", fwd_hbm, fwd_ref),
            ("adj", adj_hbm, adj_ref),
            ("tiles", tiles_hbm, tiles_ref),
            ("links", links_hbm, links_ref),
            ("omega", omega_hbm, omega_ref),
            ("mass", mass_hbm, mass_ref),
        )
    ):
        loads[name] = pltpu.make_async_copy(source, target, load_sem.at[at])
        loads[name].start()

    def raw_copy(chunk):
        rows = pl.ds(chunk * CHUNK, CHUNK)
        return pltpu.make_async_copy(curl_hbm.at[rows], raw.at[rows], raw_sem.at[chunk])

    for chunk in range(blocks // CHUNK):
        raw_copy(chunk).start()

    partners = []
    for bit in range(rounds):
        mask = 2**bit
        partners.append((freq, dom + mask * (1 - 2 * ((dom // mask) % 2))))
    others = [(lax.rem(freq + step, peers), dom) for step in range(1, peers)]

    barrier = pltpu.get_barrier_semaphore()
    for device in partners + others:
        pl.semaphore_signal(barrier, inc=1, device_id=device, device_id_type=MESH)

    for system, (name, ref) in enumerate((("fwd", fwd_ref), ("adj", adj_ref))):
        loads[name].wait()
        for f in range(count):
            for c in range(4):
                first[:, row_of(count, system, f, c), :] = ref[f, c]

    pieces = 2
    span = tiles // pieces
    group = min(UNROLL, span)

    def push(send, ext, phase, bit, piece):
        rows = bit * tiles + piece * span
        copy = pltpu.make_async_remote_copy(
            src_ref=send.at[pl.ds(rows, span)],
            dst_ref=ext.at[pl.ds(blocks + rows, span)],
            send_sem=send_sem.at[phase, bit, piece],
            recv_sem=recv_sem.at[phase, bit, piece],
            device_id=partners[bit],
            device_id_type=MESH,
        )
        copy.start()
        return copy

    loads["tiles"].wait()
    copies = []
    for bit in reversed(range(rounds)):
        for piece in range(pieces):
            for tile in range(piece * span, (piece + 1) * span):
                send_one[bit * tiles + tile] = first[tiles_ref[bit, tile]]
            if len(copies) == 0:
                pl.semaphore_wait(barrier, len(partners) + len(others))
            copies.append(push(send_one, ext_one, 0, bit, piece))
    ext_one[pl.ds(0, blocks)] = first[...]

    for name in ("links", "omega", "mass"):
        loads[name].wait()
    place = lax.broadcasted_iota(jnp.int32, (half, size), 0)
    place = lax.rem(place // 2, count)
    omega = jnp.zeros((half, size), jnp.float32)
    for f in range(count):
        omega = jnp.where(place == f, omega_ref[f], omega)
    for row in range(blocks):
        weight[row] = omega * mass_ref[pl.ds(row, 1), :]

    for chunk in range(blocks // CHUNK):
        raw_copy(chunk).wait()

        def cut(step, carry):
            row = chunk * CHUNK + step
            for link in range(links):
                high, low = split(raw[row, link].T)
                if link == 0:
                    parts_own[row, :, pl.ds(0, size)] = high
                    parts_own[row, :, pl.ds(size, size)] = low
                else:
                    rows = pl.ds((link - 1) * size, size)
                    parts[row, rows, pl.ds(0, size)] = high
                    parts[row, rows, pl.ds(size, size)] = low
            return carry

        lax.fori_loop(0, CHUNK, cut, 0)

    def stacked(value):
        return jnp.concatenate(split(value), axis=0)

    def folded(product):
        product = product[:width] + product[width:]
        return product[:, :size] + product[:, size:]

    def times(left, right):
        return jnp.dot(left, right, preferred_element_type=jnp.float32)

    def paired(one_left, two_left, one_right, two_right):
        blank = jnp.zeros_like(one_left)
        upper = jnp.concatenate([one_left, blank], axis=1)
        lower = jnp.concatenate([blank, two_left], axis=1)
        product = times(
            jnp.concatenate([upper, lower], axis=0),
            jnp.concatenate([one_right, two_right], axis=0),
        )
        return folded(product[: 2 * width]), folded(product[2 * width :])

    def own_blocks(field):
        def body(step, carry):
            for inner in range(0, UNROLL, 2):
                row = step * UNROLL + inner
                near[row], near[row + 1] = paired(
                    stacked(field[row]),
                    stacked(field[row + 1]),
                    parts_own[row],
                    parts_own[row + 1],
                )
            return carry

        lax.fori_loop(0, blocks // UNROLL, body, 0)

    def close(row, field, curl):
        value = field[row]
        turned = jnp.concatenate([-value[half:], value[:half]], axis=0)
        scale = weight[row]
        return value, curl + near[row] + jnp.concatenate([scale, scale], axis=0) * turned

    def operate(row, field, ext):
        gathered = [ext[links_ref[link, row]] for link in range(1, links)]
        left = stacked(jnp.concatenate(gathered, axis=1))
        return close(row, field, folded(times(left, parts[row])))

    def operate_two(row, field, ext):
        depth = (links - 2) * size
        curls = []
        for at in (row, row + 1):
            gathered = [ext[links_ref[link, at]] for link in range(1, links - 1)]
            left = stacked(jnp.concatenate(gathered, axis=1))
            curls.append(folded(times(left, parts[at, pl.ds(0, depth)])))
        last = paired(
            stacked(ext[links_ref[links - 1, row]]),
            stacked(ext[links_ref[links - 1, row + 1]]),
            parts[row, pl.ds(depth, size)],
            parts[row + 1, pl.ds(depth, size)],
        )
        return [
            close(at, field, curl + extra)
            for at, curl, extra in zip((row, row + 1), curls, last)
        ]

    factors = chebyshev_factors()

    def advance(value, image):
        keep, gain = factors[0]
        left = value - image
        return left, keep * value + gain * left

    own_blocks(first)
    for copy in copies:
        copy.wait()

    copies = []
    for bit in reversed(range(rounds)[-1:]):
        for piece in range(pieces):

            def ahead(step, carry):
                for inner in range(group):
                    tile = piece * span + step * group + inner
                    done = advance(*operate(tiles_ref[bit, tile], first, ext_one))
                    send_two[bit * tiles + tile] = done[1]
                return carry

            lax.fori_loop(0, span // group, ahead, 0)
            copies.append(push(send_two, ext_two, 1, bit, piece))

    def one(step, carry):
        for inner in range(0, UNROLL, 2):
            row = step * UNROLL + inner
            for at, pair in enumerate(operate_two(row, first, ext_one)):
                left, value = advance(*pair)
                resid[row + at] = left
                second[row + at] = value
        return carry

    lax.fori_loop(0, blocks // UNROLL, one, 0)
    for bit in reversed(range(rounds)[:-1]):
        for piece in range(pieces):
            for tile in range(piece * span, (piece + 1) * span):
                send_two[bit * tiles + tile] = second[tiles_ref[bit, tile]]
            copies.append(push(send_two, ext_two, 1, bit, piece))
    ext_two[pl.ds(0, blocks)] = second[...]
    own_blocks(second)
    for copy in copies:
        copy.wait()

    def two(step, carry):
        keep, gain = factors[1]
        for inner in range(0, UNROLL, 2):
            start = step * UNROLL + inner
            for at, (value, image) in enumerate(operate_two(start, second, ext_two)):
                row = start + at
                left = resid[row] - image
                done = (first[row] + value) + (keep * value + gain * left)
                total[row] = done
                crossed = jnp.concatenate(
                    [done[half + half // 2 :], done[half : half + half // 2]], axis=0
                )
                term = omega * done[:half] * crossed
                terms[freq, pl.ds(row, 1), :] = jnp.sum(term, axis=0, keepdims=True)
        return carry

    lax.fori_loop(0, blocks // UNROLL, two, 0)

    copies = []
    for step in range(1, peers):
        copy = pltpu.make_async_remote_copy(
            src_ref=terms.at[freq],
            dst_ref=terms.at[freq],
            send_sem=term_send_sem.at[step],
            recv_sem=term_recv_sem.at[step],
            device_id=others[step - 1],
            device_id_type=MESH,
        )
        copy.start()
        copies.append(copy)
    for system, ref in enumerate((fwd_ref, adj_ref)):
        for f in range(count):
            for c in range(4):
                ref[f, c] = total[:, row_of(count, system, f, c), :]
    stores = []
    for at, (source, target) in enumerate(((fwd_ref, fwd_out), (adj_ref, adj_out))):
        stores.append(pltpu.make_async_copy(source, target, load_sem.at[6 + at]))
        stores[-1].start()
    for copy in copies:
        copy.wait()
    whole = terms[0]
    for peer in range(1, peers):
        whole = whole + terms[peer]
    mass_ref[...] = whole
    stores.append(pltpu.make_async_copy(mass_ref, edge_out, load_sem.at[8]))
    stores[-1].start()
    for copy in stores:
        copy.wait()


def finish(
    scale,
    fwd_hbm,
    adj_hbm,
    edge_hbm,
    cells_hbm,
    cond_hbm,
    fwd_out,
    adj_out,
    model_out,
    edge_ref,
    cells_ref,
    cond_ref,
    fwd_ref,
    adj_ref,
    copy_sem,
):
    pairs = (
        (edge_hbm, edge_ref),
        (cells_hbm, cells_ref),
        (cond_hbm, cond_ref),
        (fwd_hbm, fwd_ref),
        (adj_hbm, adj_ref),
        (fwd_ref, fwd_out),
        (adj_ref, adj_out),
    )
    copies = [pltpu.make_async_copy(*pair, copy_sem.at[at]) for at, pair in enumerate(pairs)]
    for copy in copies[:5]:
        copy.start()
    for copy in copies[:5]:
        copy.wait()
    for copy in copies[5:]:
        copy.start()

    blocks, size = edge_ref.shape
    corners, cells = cells_ref.shape
    shift = size.bit_length() - 1
    sums = []
    for column in range(cells // size):
        acc = jnp.zeros((1, size), jnp.float32)
        for start in range(0, corners, 8):
            rows = min(8, corners - start)
            ids = cells_ref[pl.ds(start, rows), pl.ds(column * size, size)]
            if rows < 8:
                ids = jnp.concatenate([ids, jnp.full((8 - rows, size), -1, jnp.int32)], axis=0)
            block = ids >> shift
            lane = ids & (size - 1)
            found = jnp.zeros((8, size), jnp.float32)
            for row in range(blocks):
                values = jnp.broadcast_to(edge_ref[pl.ds(row, 1), :], (8, size))
                got = jnp.take_along_axis(values, lane, axis=1, mode="promise_in_bounds")
                found = jnp.where(block == row, got, found)
            acc = acc + jnp.sum(found, axis=0, keepdims=True)
        sums.append(acc)
    grad = jnp.concatenate(sums, axis=0) * scale
    model_out[...] = cond_ref[...] - 0.5 * grad / jnp.sqrt(grad * grad + 1.0)
    for copy in copies[5:]:
        copy.wait()


def local(
    fwd_source,
    adj_source,
    curl_blocks,
    block_links,
    tile_lists,
    edge_mass,
    omega,
    cell_edges,
    log_cond,
):
    count, _, blocks, size = fwd_source.shape
    peers = lax.axis_size("freq")
    width = 8 * count
    rounds, tiles = tile_lists.shape
    sent = rounds * tiles
    links = block_links.shape[1]
    cells = log_cond.shape[0]
    cond = log_cond.reshape(cells // size, size)
    f32, bf16 = jnp.float32, jnp.bfloat16
    vmem = pl.BlockSpec(memory_space=pltpu.VMEM)
    hbm = pl.BlockSpec(memory_space=pltpu.HBM)
    fields, adjoint, edge = pl.pallas_call(
        functools.partial(kernel, peers),
        out_shape=(
            jax.ShapeDtypeStruct(fwd_source.shape, f32),
            jax.ShapeDtypeStruct(adj_source.shape, f32),
            jax.ShapeDtypeStruct((blocks, size), f32),
        ),
        in_specs=[hbm] * 7,
        out_specs=(hbm,) * 3,
        scratch_shapes=[
            pltpu.SMEM((links, blocks), jnp.int32),
            pltpu.SMEM((rounds, tiles), jnp.int32),
            pltpu.SMEM((count,), f32),
            pltpu.VMEM(fwd_source.shape, f32),
            pltpu.VMEM(adj_source.shape, f32),
            pltpu.VMEM((blocks, size), f32),
            pltpu.VMEM(curl_blocks.shape, f32),
            pltpu.VMEM((blocks, size, 2 * size), bf16),
            pltpu.VMEM((blocks, (links - 1) * size, 2 * size), bf16),
            pltpu.VMEM((blocks, width, size), f32),
            pltpu.VMEM((blocks, width // 2, size), f32),
            pltpu.VMEM((blocks, width, size), f32),
            pltpu.VMEM((blocks, width, size), f32),
            pltpu.VMEM((blocks, width, size), f32),
            pltpu.VMEM((blocks, width, size), f32),
            pltpu.VMEM((blocks + sent, width, size), f32),
            pltpu.VMEM((blocks + sent, width, size), f32),
            pltpu.VMEM((sent, width, size), f32),
            pltpu.VMEM((sent, width, size), f32),
            pltpu.VMEM((peers, blocks, size), f32),
            pltpu.SemaphoreType.DMA((9,)),
            pltpu.SemaphoreType.DMA((blocks // CHUNK,)),
            pltpu.SemaphoreType.DMA((2, rounds, 2)),
            pltpu.SemaphoreType.DMA((2, rounds, 2)),
            pltpu.SemaphoreType.DMA((peers,)),
            pltpu.SemaphoreType.DMA((peers,)),
        ],
        compiler_params=pltpu.CompilerParams(
            collective_id=0, has_side_effects=True, vmem_limit_bytes=VMEM
        ),
    )(
        block_links.T,
        tile_lists,
        omega,
        fwd_source,
        adj_source,
        curl_blocks,
        edge_mass,
    )
    scale = 1.0 / (24.0 * count * peers) ** 0.5
    fwd_field, adj_field, model = pl.pallas_call(
        functools.partial(finish, scale),
        out_shape=(
            jax.ShapeDtypeStruct(fwd_source.shape, f32),
            jax.ShapeDtypeStruct(adj_source.shape, f32),
            jax.ShapeDtypeStruct(cond.shape, f32),
        ),
        in_specs=[hbm] * 5,
        out_specs=(hbm, hbm, vmem),
        scratch_shapes=[
            pltpu.VMEM((blocks, size), f32),
            pltpu.VMEM(cell_edges.shape, jnp.int32),
            pltpu.VMEM(cond.shape, f32),
            pltpu.VMEM(fwd_source.shape, f32),
            pltpu.VMEM(adj_source.shape, f32),
            pltpu.SemaphoreType.DMA((7,)),
        ],
        compiler_params=pltpu.CompilerParams(vmem_limit_bytes=VMEM),
    )(fields, adjoint, edge, cell_edges, cond)
    return fwd_field, adj_field, model.reshape(cells)


def solution(mesh):
    in_specs = (
        P("freq", None, "dom", None),
        P("freq", None, "dom", None),
        P("dom", None, None, None),
        P("dom", None),
        P("dom", None),
        P("dom", None),
        P("freq"),
        P(None, "dom"),
        P("dom"),
    )
    out_specs = (P("freq", None, "dom", None), P("freq", None, "dom", None), P("dom"))
    return jax.shard_map(local, mesh=mesh, in_specs=in_specs, out_specs=out_specs, check_vma=False)
```
